512 devices in a mesh: freq: 8 (over y), elem: 64 (over z, x, core).
Axes of the slice: x: 4, y: 8, z: 8, core: 2. Of those that a mesh axis runs over, the one named last changes fastest.
Arguments:
- history: bfloat16 [512, 65536], P('freq', 'elem'), may hold values from -6 to 6
- near_blocks: bfloat16 [8, 512, 3, 2, 128, 128], P('freq', 'elem'), may hold values from -0.21875 to 0.21875
- near_leaves: int32 [512, 3], P('elem'), may hold values from 0 to 511, as said below
- far_left: bfloat16 [8, 768, 2, 128, 128], P('freq', 'elem'), may hold values from -0.375 to 0.375
- far_right: bfloat16 [8, 768, 2, 128, 128], P('freq', 'elem'), may hold values from -0.375 to 0.375
- far_ranks: int32 [8, 768], P('freq', 'elem'), may hold values from 1 to 128, as said below
- far_targets: int32 [768], P('elem'), may hold values from 0 to 511
- far_sources: int32 [768], P('elem'), may hold values from 0 to 511
Outputs:
- field: bfloat16 [8, 2, 65536], P('freq', None, 'elem')
The draws below stay inside these ranges and needn't reach their ends.
Inputs may be any that keep to these rules, and one draw needn't show every extreme that they name: `near_leaves`: the first entry of each row is the leaf itself; every other entry lies within 8 leaves of it. `far_ranks`: at each frequency, at most 4 of the 12 tasks of one device (aligned blocks of tasks) have a rank above 64, and at the last frequency some device has exactly 4 such tasks.
All inputs are finite; a program needn't handle non-finite values.
Results may differ from the reference program's by a relative error of at most 0.0059.
Values may be sent and summed in bfloat16 or wider, within the bound.
No kernel may reach another device: no remote copies, remote signals or barrier semaphores. Data moves between devices by JAX's collectives and lax.ppermute only.
A program may use at most 64 MiB of HBM per device.

```python
import math
import jax
import jax.numpy as jnp
from jax import lax

STEPS = 512
LEAF = 128
RMAX = 128
NEAR = 3
LEAVES_DEV = 8
TASK_DEV = 12
HEAVY = 4
NF = 8
LEAVES = 512
NELEM = 65536
TASKS = 768


def draw_near_leaves(key, part):
    key = jax.random.fold_in(key, 5)
    keys = jax.random.split(key, 2)
    leaf_index = jnp.arange(LEAVES, dtype=jnp.int32)[:, None]
    offset = jax.random.randint(keys[0], (LEAVES, NEAR), 1, LEAVES_DEV + 1)
    offset = offset * (2 * jax.random.randint(keys[1], (LEAVES, NEAR), 0, 2) - 1)
    offset = jnp.where(jnp.arange(NEAR, dtype=jnp.int32)[None, :] == 0, 0, offset)
    target = leaf_index + offset
    target = jnp.where((target < 0) | (target >= LEAVES), leaf_index - offset, target)
    return target.astype(jnp.int32)


def draw_far_ranks(key, part):
    key = jax.random.fold_in(key, 7)
    keys = jax.random.split(key, 5)
    groups = TASKS // TASK_DEV
    freq_index = jnp.arange(NF, dtype=jnp.int32)[:, None]
    ceiling = HEAVY * (freq_index + 1) // NF
    heavy_count = jax.random.randint(keys[0], (NF, groups), 0, 1 << 20) % (ceiling + 1)
    chosen = jax.random.randint(keys[1], (), 0, groups)
    forced = (freq_index == NF - 1) & (jnp.arange(groups, dtype=jnp.int32)[None, :] == chosen)
    heavy_count = jnp.where(forced, HEAVY, heavy_count)
    scores = jax.random.randint(keys[2], (NF, groups, TASK_DEV), 0, 1 << 16) * TASK_DEV + jnp.arange(TASK_DEV, dtype=jnp.int32)
    position = jnp.argsort(jnp.argsort(scores, axis=-1), axis=-1)
    heavy_value = jax.random.randint(keys[3], (NF, groups, TASK_DEV), RMAX // 2 + 1, RMAX + 1)
    light_value = jax.random.randint(keys[4], (NF, groups, TASK_DEV), 1, RMAX // 2 + 1)
    value = jnp.where(position < heavy_count[:, :, None], heavy_value, light_value)
    forced_cell = forced[:, :, None]
    value = jnp.where(forced_cell & (position == 0), RMAX, value)
    value = jnp.where(forced_cell & (position == TASK_DEV - 1), 1, value)
    return value.reshape(NF, TASKS).astype(jnp.int32)


def plant(array, own_key, low, high):
    extent = array.shape
    index_at = [jax.random.randint(jax.random.fold_in(own_key, axis), (), 0, extent[axis]) for axis in range(len(extent))]
    array = array.at[tuple(index_at)].set(low)
    longest = extent.index(max(extent))
    index_at[longest] = (index_at[longest] + 1) % extent[longest]
    return array.at[tuple(index_at)].set(high)


def block_levels(stream_key, shape, pieces, smallest, top_value):
    def one(axis_at, shards_of):
        steps = jax.random.uniform(jax.random.fold_in(jax.random.fold_in(stream_key, 6), axis_at), (shards_of,), jnp.float32, smallest / len(pieces), top_value / len(pieces))
        return jnp.repeat(jnp.exp(steps), shape[axis_at] // shards_of).reshape((-1,) + (1,) * (len(shape) - axis_at - 1))

    factor_of = one(*pieces[0])
    for cut in pieces[1:]:
        factor_of = factor_of * one(*cut)
    return factor_of


def scatter_about(stream_key, shape, scale, most, pieces=(), kind=jnp.bfloat16):
    gain = block_levels(stream_key, shape, pieces, -0.22, 0.18) if pieces else 1.0
    drawn = jax.random.normal(stream_key, shape, jnp.float32) * scale * gain
    return jnp.minimum(jnp.maximum(drawn, -most), most).astype(kind)


def setup_inputs(seed: int = 0) -> dict:
    seeds = jax.random.split(jax.random.key(seed), 9)
    history = scatter_about(seeds[0], (STEPS, NELEM), 1.0, 6.0, ((0, 8), (1, 64)))
    near_blocks = scatter_about(seeds[1], (NF, LEAVES, NEAR, 2, LEAF, LEAF), (2 * NEAR * LEAF) ** -0.5, 0.21875, ((0, 8), (1, 64)))
    near_leaves = draw_near_leaves(jax.random.fold_in(seeds[8], 71), 0)
    far_left = scatter_about(seeds[3], (NF, TASKS, 2, LEAF, RMAX), (2 * RMAX) ** -0.5, 0.375, ((0, 8), (1, 64)))
    far_right = scatter_about(seeds[4], (NF, TASKS, 2, LEAF, RMAX), (2 * LEAF) ** -0.5, 0.375, ((0, 8), (1, 64)))
    far_ranks = draw_far_ranks(jax.random.fold_in(seeds[8], 71), 0)
    far_targets = plant(jax.random.randint(seeds[6], (TASKS,), 0, LEAVES), jax.random.fold_in(seeds[6], 1), 0, LEAVES - 1).astype(jnp.int32)
    far_sources = plant(jax.random.randint(seeds[7], (TASKS,), 0, LEAVES), jax.random.fold_in(seeds[7], 1), 0, LEAVES - 1).astype(jnp.int32)
    return {"history": history, "near_blocks": near_blocks, "near_leaves": near_leaves, "far_left": far_left, "far_right": far_right, "far_ranks": far_ranks, "far_targets": far_targets, "far_sources": far_sources}


fall_total = 0.25

def dft_weights(freq_start, freq_count, step_start, step_count, total_freq, total_steps):
    freq_index = (freq_start + jnp.arange(freq_count, dtype=jnp.int32)) * (total_steps // total_freq) + 1
    step_index = step_start + jnp.arange(step_count, dtype=jnp.int32)
    phase_index = freq_index[:, None] * step_index[None, :] % total_steps
    angles = 2.0 * math.pi / total_steps * phase_index.astype(jnp.float32)
    damping = fall_total ** (step_index.astype(jnp.float32) / total_steps) / math.sqrt(total_steps)
    return jnp.stack([damping * jnp.cos(angles), -damping * jnp.sin(angles)], 1).astype(jnp.bfloat16)

def product(form, first_op, second_op):
    return jnp.einsum(form, first_op.astype(jnp.float32), second_op.astype(jnp.float32), precision=lax.Precision.HIGHEST)

def far_terms(leaf_view, left_factor, right_factor, sources, task_ranks):
    picked = leaf_view[:, sources]
    coeff_re = product('tjr,tj->tr', right_factor[:, 0], picked[0]) - product('tjr,tj->tr', right_factor[:, 1], picked[1])
    coeff_im = product('tjr,tj->tr', right_factor[:, 0], picked[1]) + product('tjr,tj->tr', right_factor[:, 1], picked[0])
    inside = jnp.arange(right_factor.shape[-1], dtype=jnp.int32)[None, :] < task_ranks[:, None]
    coeff_re = lax.optimization_barrier(jnp.where(inside, coeff_re, 0.0).astype(jnp.bfloat16)).astype(jnp.float32)
    coeff_im = lax.optimization_barrier(jnp.where(inside, coeff_im, 0.0).astype(jnp.bfloat16)).astype(jnp.float32)
    out_re = product('tir,tr->ti', left_factor[:, 0], coeff_re) - product('tir,tr->ti', left_factor[:, 1], coeff_im)
    out_im = product('tir,tr->ti', left_factor[:, 0], coeff_im) + product('tir,tr->ti', left_factor[:, 1], coeff_re)
    return jnp.stack([out_re, out_im], 1)

def reference(history, near_blocks, near_leaves, far_left, far_right, far_ranks, far_targets, far_sources):
    weights = dft_weights(0, NF, 0, STEPS, NF, STEPS)
    spectrum = product('fct,te->fce', weights, history).astype(jnp.bfloat16)
    spectrum = lax.optimization_barrier(spectrum)
    outputs = []
    for freq_index in range(NF):
        leaf_view = spectrum[freq_index].astype(jnp.float32).reshape(2, LEAVES, LEAF)
        near_view = leaf_view[:, near_leaves]
        blocks = near_blocks[freq_index]
        near_re = product('lnij,lnj->li', blocks[:, :, 0], near_view[0]) - product('lnij,lnj->li', blocks[:, :, 1], near_view[1])
        near_im = product('lnij,lnj->li', blocks[:, :, 0], near_view[1]) + product('lnij,lnj->li', blocks[:, :, 1], near_view[0])
        contrib = far_terms(leaf_view, far_left[freq_index], far_right[freq_index], far_sources, far_ranks[freq_index])
        far_part = jnp.zeros((LEAVES, 2, LEAF), jnp.float32).at[far_targets].add(contrib)
        combined = jnp.stack([near_re, near_im], 1) + far_part
        outputs.append(combined.transpose(1, 0, 2).reshape(2, NELEM).astype(jnp.bfloat16))
    return jnp.stack(outputs, 0)
```

```python
import math

import jax
import jax.numpy as jnp
from jax import lax
from jax.sharding import PartitionSpec as P

fall_total = 0.25


def dft_weights(freq_count, step_start, step_count, total_freq, total_steps):
    freq_index = jnp.arange(freq_count, dtype=jnp.int32) * (total_steps // total_freq) + 1
    step_index = step_start + jnp.arange(step_count, dtype=jnp.int32)
    phase_index = freq_index[:, None] * step_index[None, :] % total_steps
    angles = 2.0 * math.pi / total_steps * phase_index.astype(jnp.float32)
    damping = fall_total ** (step_index.astype(jnp.float32) / total_steps) / math.sqrt(total_steps)
    return jnp.stack([damping * jnp.cos(angles), -damping * jnp.sin(angles)], 1).astype(
        jnp.bfloat16
    )


def product(form, first_op, second_op):
    return jnp.einsum(form, first_op, second_op, preferred_element_type=jnp.float32)


def far_terms(leaf_view, left_factor, right_factor, sources, task_ranks):
    picked = leaf_view[sources]
    coeff_re = product("tjr,tj->tr", right_factor[:, 0], picked[:, 0]) - product(
        "tjr,tj->tr", right_factor[:, 1], picked[:, 1]
    )
    coeff_im = product("tjr,tj->tr", right_factor[:, 0], picked[:, 1]) + product(
        "tjr,tj->tr", right_factor[:, 1], picked[:, 0]
    )
    inside = jnp.arange(right_factor.shape[-1], dtype=jnp.int32)[None, :] < task_ranks[:, None]
    coeff_re = jnp.where(inside, coeff_re, 0.0).astype(jnp.bfloat16)
    coeff_im = jnp.where(inside, coeff_im, 0.0).astype(jnp.bfloat16)
    out_re = product("tir,tr->ti", left_factor[:, 0], coeff_re) - product(
        "tir,tr->ti", left_factor[:, 1], coeff_im
    )
    out_im = product("tir,tr->ti", left_factor[:, 0], coeff_im) + product(
        "tir,tr->ti", left_factor[:, 1], coeff_re
    )
    return jnp.stack([out_re, out_im], 1)


def per_device(
    history, near_blocks, near_leaves, far_left, far_right, far_ranks, far_targets, far_sources
):
    freq_groups = lax.axis_size("freq")
    elem_groups = lax.axis_size("elem")
    local_freq = far_ranks.shape[0]
    total_freq = local_freq * freq_groups
    steps_here = history.shape[0]
    total_steps = steps_here * freq_groups
    leaf_size = near_blocks.shape[-1]
    local_leaves = near_blocks.shape[1]
    all_leaves = local_leaves * elem_groups
    first_step = lax.axis_index("freq") * steps_here
    weights = dft_weights(total_freq, first_step, steps_here, total_freq, total_steps)
    partial = product("fct,te->fce", weights, history)
    partial = partial.reshape(total_freq, 2 * local_leaves, leaf_size)
    shares = lax.all_to_all(partial, "freq", 0, 0, tiled=True)
    spectrum = jnp.sum(shares, 0).astype(jnp.bfloat16)
    copies = jnp.broadcast_to(spectrum[None], (elem_groups,) + spectrum.shape)
    gathered = lax.all_to_all(copies, "elem", 0, 0, tiled=True)
    leaf_view = gathered.reshape(elem_groups, 2, local_leaves, leaf_size).transpose(0, 2, 1, 3)
    leaf_view = leaf_view.reshape(all_leaves, 2, leaf_size)
    near_view = leaf_view[near_leaves]
    blocks = near_blocks[0]
    near_re = product("lnij,lnj->li", blocks[:, :, 0], near_view[:, :, 0]) - product(
        "lnij,lnj->li", blocks[:, :, 1], near_view[:, :, 1]
    )
    near_im = product("lnij,lnj->li", blocks[:, :, 0], near_view[:, :, 1]) + product(
        "lnij,lnj->li", blocks[:, :, 1], near_view[:, :, 0]
    )
    contrib = far_terms(leaf_view, far_left[0], far_right[0], far_sources, far_ranks[0])
    spread_terms = jnp.zeros((all_leaves, 2, leaf_size), jnp.float32).at[far_targets].add(contrib)
    spread_terms = spread_terms.astype(jnp.bfloat16).reshape(elem_groups, 2 * local_leaves, leaf_size)
    arrived = lax.all_to_all(spread_terms, "elem", 0, 0, tiled=True)
    far_part = jnp.sum(arrived.astype(jnp.float32), 0).reshape(local_leaves, 2, leaf_size)
    combined = jnp.stack([near_re, near_im], 1) + far_part
    return combined.transpose(1, 0, 2).reshape(1, 2, -1).astype(jnp.bfloat16)


def solution(mesh):
    in_specs = (
        P("freq", "elem"),
        P("freq", "elem", None, None, None, None),
        P("elem", None),
        P("freq", "elem", None, None, None),
        P("freq", "elem", None, None, None),
        P("freq", "elem"),
        P("elem"),
        P("elem"),
    )
    out_specs = P("freq", None, "elem")
    return jax.shard_map(
        per_device, mesh=mesh, in_specs=in_specs, out_specs=out_specs, check_vma=False
    )
```

```python
import functools
import math

import jax
import jax.numpy as jnp
from jax import lax
from jax.experimental import pallas as pl
from jax.experimental.pallas import tpu as pltpu
from jax.sharding import Mesh
from jax.sharding import PartitionSpec as P

fall_total = 0.25
CORES = 2
GROUP = 8
LIMIT = 32 * 1024 * 1024


def dot(first_op, second_op, transposed=False):
    dims = (((1,), (1 if transposed else 0,)), ((), ()))
    return lax.dot_general(first_op, second_op, dims, preferred_element_type=jnp.float32)


def turn(direct, crossed):
    swapped = jnp.concatenate([-crossed[GROUP:], crossed[:GROUP]], 0)
    return direct + swapped


def partial_kernel(total_freq, total_steps, first_ref, history_ref, out_ref):
    steps = history_ref.shape[0]
    rows = 2 * total_freq
    leaf = out_ref.shape[-1]
    leaves = history_ref.shape[1] // leaf
    row = lax.broadcasted_iota(jnp.int32, (rows, steps), 0)
    step = first_ref[0] + lax.broadcasted_iota(jnp.int32, (rows, steps), 1)
    freq = (row >> 1) * (total_steps // total_freq) + 1
    phase = (freq * step + (row & 1) * (total_steps // 4)) & (total_steps - 1)
    angle = 2.0 * math.pi / total_steps * phase.astype(jnp.float32)
    damping = jnp.exp(step.astype(jnp.float32) * (math.log(fall_total) / total_steps))
    weights = (damping * jnp.cos(angle) / math.sqrt(total_steps)).astype(jnp.bfloat16)
    part = dot(weights, history_ref[...])
    for l in range(leaves):
        out_ref[pl.ds(l, rows, stride=leaves), :] = part[:, l * leaf : (l + 1) * leaf]


def far_kernel(tasks, pick_ref, gathered_ref, ranks_ref, right_ref, left_ref, out_ref):
    picked = dot(pick_ref[...], gathered_ref[...]).astype(jnp.bfloat16)
    half = picked.shape[0] // 2
    pair = jnp.concatenate([picked[:half], picked[half:]], 1)
    leaf = left_ref.shape[-1]
    own = lax.broadcasted_iota(jnp.int32, (2 * GROUP, leaf), 0) % GROUP
    lane = lax.broadcasted_iota(jnp.int32, (2 * GROUP, leaf), 1)
    for start in range(0, tasks, GROUP):
        rows = slice(2 * start, 2 * start + 2 * GROUP)
        here = range(start, min(start + GROUP, tasks))
        coeff = jnp.zeros((2 * GROUP, leaf), jnp.float32)
        for t in here:
            coeff = jnp.where(own == t - start, dot(pair[rows], right_ref[t]), coeff)
        coeff = jnp.where(lane < ranks_ref[rows, :], coeff, 0.0).astype(jnp.bfloat16)
        direct = jnp.zeros((2 * GROUP, leaf), jnp.float32)
        crossed = jnp.zeros((2 * GROUP, leaf), jnp.float32)
        for t in here:
            both = dot(coeff, left_ref[t], True)
            direct = jnp.where(own == t - start, both[:, :leaf], direct)
            crossed = jnp.where(own == t - start, both[:, leaf:], crossed)
        out_ref[rows, :] = turn(direct, crossed).astype(jnp.bfloat16)


def near_kernel(pick_ref, gathered_ref, blocks_ref, out_ref):
    leaves, near = blocks_ref.shape[:2]
    leaf = blocks_ref.shape[-1]
    picked = dot(pick_ref[...], gathered_ref[...]).astype(jnp.bfloat16)
    own = lax.broadcasted_iota(jnp.int32, (2 * GROUP, leaf), 0) % GROUP
    direct = jnp.zeros((2 * GROUP, leaf), jnp.float32)
    crossed = jnp.zeros((2 * GROUP, leaf), jnp.float32)
    for n in range(near):
        view = picked[2 * GROUP * n : 2 * GROUP * (n + 1)]
        for l in range(leaves):
            both = dot(view, blocks_ref[l, n], True)
            direct = direct + jnp.where(own == l, both[:, :leaf], 0.0)
            crossed = crossed + jnp.where(own == l, both[:, leaf:], 0.0)
    out_ref[...] = turn(direct, crossed)


def call(kernel, shape, dtype, smem=0):
    def run(*operands):
        return pl.pallas_call(
            kernel,
            out_shape=jax.ShapeDtypeStruct(shape, dtype),
            in_specs=[
                pl.BlockSpec(memory_space=pltpu.SMEM if i < smem else pltpu.VMEM)
                for i in range(len(operands))
            ],
            out_specs=pl.BlockSpec(memory_space=pltpu.VMEM),
            compiler_params=pltpu.CompilerParams(vmem_limit_bytes=LIMIT),
        )(*operands)

    return run


def per_device(
    history, near_blocks, near_leaves, far_left, far_right, far_ranks, far_targets, far_sources
):
    freq_groups = lax.axis_size("freq")
    chips = lax.axis_size("chip")
    core = lax.axis_index("core")
    total_freq = far_ranks.shape[0] * freq_groups
    steps_here = history.shape[0]
    total_steps = steps_here * freq_groups
    leaf = near_blocks.shape[-1]
    leaves = near_blocks.shape[1]
    near = near_blocks.shape[2]
    tasks = far_ranks.shape[1]
    slots = -(-tasks // GROUP) * GROUP

    first_step = lax.axis_index("freq") * steps_here
    partial = call(
        functools.partial(partial_kernel, total_freq, total_steps),
        (2 * total_freq * leaves, leaf),
        jnp.float32,
        1,
    )(first_step.astype(jnp.int32)[None], history)
    shares = lax.all_to_all(
        partial.reshape(total_freq, 2 * leaves, leaf), "freq", 0, 0, tiled=True
    )
    spectrum = jnp.sum(shares, 0).astype(jnp.bfloat16)
    copies = jnp.broadcast_to(spectrum[None], (chips,) + spectrum.shape)
    same_core = lax.all_to_all(copies, "chip", 0, 0, tiled=True)
    gathered = lax.all_gather(same_core, "core", axis=0, tiled=False)
    gathered = gathered.reshape(CORES * chips * 2 * leaves, leaf)

    at = jnp.arange(gathered.shape[0], dtype=jnp.int32)
    at_leaf = (at // (2 * leaves) % chips * CORES + at // (2 * leaves * chips)) * leaves + at % leaves
    at_part = at // leaves % 2

    row = jnp.arange(2 * slots, dtype=jnp.int32)
    row_part = row // GROUP % 2

    def by_row(values, fill):
        padded = jnp.concatenate([values, jnp.full((slots - tasks,), fill, jnp.int32)])
        grouped = padded.reshape(slots // GROUP, 1, GROUP)
        return jnp.broadcast_to(grouped, (slots // GROUP, 2, GROUP)).reshape(-1)

    hit = by_row(far_sources, -1)[:, None] == at_leaf[None, :]
    same = row_part[:, None] == at_part[None, :]
    sign = jnp.where(row_part == 0, -1.0, 1.0)[:, None]
    pick_far = jnp.concatenate(
        [jnp.where(hit & same, 1.0, 0.0), jnp.where(hit & ~same, sign, 0.0)], 0
    ).astype(jnp.bfloat16)
    ranks = jnp.broadcast_to(by_row(far_ranks[0], 0)[:, None], (2 * slots, leaf))
    contrib = call(
        functools.partial(far_kernel, tasks), (2 * slots, leaf), jnp.bfloat16
    )(
        pick_far,
        gathered,
        ranks,
        far_right[0].reshape(tasks, 2 * leaf, leaf),
        far_left[0].reshape(tasks, 2 * leaf, leaf),
    )

    both_targets = lax.all_gather(far_targets, "core", axis=0, tiled=False)
    both_terms = lax.all_gather(contrib, "core", axis=0, tiled=True)
    goal = jnp.concatenate([by_row(both_targets[i], -1) for i in range(CORES)])
    out_row = jnp.arange(chips * 2 * leaves, dtype=jnp.int32)
    out_leaf = (out_row // (2 * leaves) * CORES + core) * leaves + out_row % leaves
    out_part = out_row // leaves % 2
    place = (out_leaf[:, None] == goal[None, :]) & (
        out_part[:, None] == jnp.tile(row_part, CORES)[None, :]
    )
    spread = dot(place.astype(jnp.bfloat16), both_terms).astype(jnp.bfloat16)
    arrived = lax.all_to_all(
        spread.reshape(chips, 2 * leaves, leaf), "chip", 0, 0, tiled=True
    )

    wanted = jnp.broadcast_to(near_leaves.T[:, None, :], (near, 2, leaves)).reshape(-1)
    wanted_part = jnp.arange(near * 2 * leaves, dtype=jnp.int32) // leaves % 2
    pick_near = (wanted[:, None] == at_leaf[None, :]) & (wanted_part[:, None] == at_part[None, :])
    near_field = call(near_kernel, (2 * leaves, leaf), jnp.float32)(
        pick_near.astype(jnp.bfloat16),
        gathered,
        near_blocks[0].reshape(leaves, near, 2 * leaf, leaf),
    )

    field = near_field + jnp.sum(arrived.astype(jnp.float32), 0)
    return field.reshape(1, 2, leaves * leaf).astype(jnp.bfloat16)


def solution(mesh):
    freq_groups, elem_groups = mesh.devices.shape
    split = Mesh(
        mesh.devices.reshape(freq_groups, elem_groups // CORES, CORES), ("freq", "chip", "core")
    )
    elem = ("chip", "core")
    in_specs = (
        P("freq", elem),
        P("freq", elem, None, None, None, None),
        P(elem, None),
        P("freq", elem, None, None, None),
        P("freq", elem, None, None, None),
        P("freq", elem),
        P(elem),
        P(elem),
    )
    out_specs = P("freq", None, elem)
    return jax.shard_map(
        per_device, mesh=split, in_specs=in_specs, out_specs=out_specs, check_vma=False
    )
```

```python
import functools
import math

import jax
import jax.numpy as jnp
from jax import lax
from jax.experimental import pallas as pl
from jax.experimental.pallas import tpu as pltpu
from jax.sharding import Mesh
from jax.sharding import PartitionSpec as P

fall_total = 0.25
CORES = 2
GROUP = 8
LIMIT = 32 * 1024 * 1024


def dot(first_op, second_op, transposed=False):
    dims = (((1,), (1 if transposed else 0,)), ((), ()))
    return lax.dot_general(first_op, second_op, dims, preferred_element_type=jnp.float32)


def turn(direct, crossed):
    swapped = jnp.concatenate([-crossed[GROUP:], crossed[:GROUP]], 0)
    return direct + swapped


def rotated(size):
    return [(i + size // 2) % size for i in range(size)]


def partial_kernel(total_freq, total_steps, first_ref, history_ref, out_ref):
    steps = history_ref.shape[0]
    rows = 2 * total_freq
    leaf = out_ref.shape[-1]
    leaves = history_ref.shape[1] // leaf
    row = lax.broadcasted_iota(jnp.int32, (rows, steps), 0)
    step = first_ref[0] + lax.broadcasted_iota(jnp.int32, (rows, steps), 1)
    freq = ((row >> 1) + total_freq // 2) % total_freq * (total_steps // total_freq) + 1
    phase = (freq * step + (row & 1) * (total_steps // 4)) & (total_steps - 1)
    angle = 2.0 * math.pi / total_steps * phase.astype(jnp.float32)
    damping = jnp.exp(step.astype(jnp.float32) * (math.log(fall_total) / total_steps))
    weights = (damping * jnp.cos(angle) / math.sqrt(total_steps)).astype(jnp.bfloat16)
    part = dot(weights, history_ref[...])
    for l in range(leaves):
        out_ref[pl.ds(l, rows, stride=leaves), :] = part[:, l * leaf : (l + 1) * leaf]


def far_kernel(tasks, pick_ref, gathered_ref, ranks_ref, right_ref, left_ref, out_ref):
    picked = dot(pick_ref[...], gathered_ref[...]).astype(jnp.bfloat16)
    half = picked.shape[0] // 2
    pair = jnp.concatenate([picked[:half], picked[half:]], 1)
    leaf = left_ref.shape[-1]
    own = lax.broadcasted_iota(jnp.int32, (2 * GROUP, leaf), 0) % GROUP
    lane = lax.broadcasted_iota(jnp.int32, (2 * GROUP, leaf), 1)
    for start in range(0, tasks, GROUP):
        rows = slice(2 * start, 2 * start + 2 * GROUP)
        here = range(start, min(start + GROUP, tasks))
        coeff = jnp.zeros((2 * GROUP, leaf), jnp.float32)
        for t in here:
            coeff = jnp.where(own == t - start, dot(pair[rows], right_ref[t]), coeff)
        coeff = jnp.where(lane < ranks_ref[rows, :], coeff, 0.0).astype(jnp.bfloat16)
        direct = jnp.zeros((2 * GROUP, leaf), jnp.float32)
        crossed = jnp.zeros((2 * GROUP, leaf), jnp.float32)
        for t in here:
            both = dot(coeff, left_ref[t], True)
            direct = jnp.where(own == t - start, both[:, :leaf], direct)
            crossed = jnp.where(own == t - start, both[:, leaf:], crossed)
        out_ref[rows, :] = turn(direct, crossed).astype(jnp.bfloat16)


def near_kernel(pick_ref, gathered_ref, blocks_ref, out_ref):
    leaves, near = blocks_ref.shape[:2]
    leaf = blocks_ref.shape[-1]
    picked = dot(pick_ref[...], gathered_ref[...]).astype(jnp.bfloat16)
    own = lax.broadcasted_iota(jnp.int32, (2 * GROUP, leaf), 0) % GROUP
    direct = jnp.zeros((2 * GROUP, leaf), jnp.float32)
    crossed = jnp.zeros((2 * GROUP, leaf), jnp.float32)
    for n in range(near):
        view = picked[2 * GROUP * n : 2 * GROUP * (n + 1)]
        for l in range(leaves):
            both = dot(view, blocks_ref[l, n], True)
            direct = direct + jnp.where(own == l, both[:, :leaf], 0.0)
            crossed = crossed + jnp.where(own == l, both[:, leaf:], 0.0)
    out_ref[...] = turn(direct, crossed)


def call(kernel, shape, dtype, smem=0):
    def run(*operands):
        return pl.pallas_call(
            kernel,
            out_shape=jax.ShapeDtypeStruct(shape, dtype),
            in_specs=[
                pl.BlockSpec(memory_space=pltpu.SMEM if i < smem else pltpu.VMEM)
                for i in range(len(operands))
            ],
            out_specs=pl.BlockSpec(memory_space=pltpu.VMEM),
            compiler_params=pltpu.CompilerParams(vmem_limit_bytes=LIMIT),
        )(*operands)

    return run


def per_device(
    history, near_blocks, near_leaves, far_left, far_right, far_ranks, far_targets, far_sources
):
    freq_groups = lax.axis_size("freq")
    chips = lax.axis_size("chip")
    core = lax.axis_index("core")
    total_freq = far_ranks.shape[0] * freq_groups
    steps_here = history.shape[0]
    total_steps = steps_here * freq_groups
    leaf = near_blocks.shape[-1]
    leaves = near_blocks.shape[1]
    near = near_blocks.shape[2]
    tasks = far_ranks.shape[1]
    slots = -(-tasks // GROUP) * GROUP

    first_step = lax.axis_index("freq") * steps_here
    partial = call(
        functools.partial(partial_kernel, total_freq, total_steps),
        (2 * total_freq * leaves, leaf),
        jnp.float32,
        1,
    )(first_step.astype(jnp.int32)[None], history)
    shares = lax.all_to_all(
        partial.reshape(total_freq, 2 * leaves, leaf),
        "freq",
        0,
        0,
        axis_index_groups=[rotated(freq_groups)],
        tiled=True,
    )
    spectrum = jnp.sum(shares, 0).astype(jnp.bfloat16)
    copies = jnp.broadcast_to(spectrum[None], (chips,) + spectrum.shape)
    same_core = lax.all_to_all(copies, "chip", 0, 0, tiled=True)
    gathered = lax.all_gather(same_core, "core", axis=0, tiled=False)
    gathered = gathered.reshape(CORES * chips * 2 * leaves, leaf)

    at = jnp.arange(gathered.shape[0], dtype=jnp.int32)
    at_leaf = (at // (2 * leaves) % chips * CORES + at // (2 * leaves * chips)) * leaves + at % leaves
    at_part = at // leaves % 2

    row = jnp.arange(2 * slots, dtype=jnp.int32)
    row_part = row // GROUP % 2

    def by_row(values, fill):
        padded = jnp.concatenate([values, jnp.full((slots - tasks,), fill, jnp.int32)])
        grouped = padded.reshape(slots // GROUP, 1, GROUP)
        return jnp.broadcast_to(grouped, (slots // GROUP, 2, GROUP)).reshape(-1)

    hit = by_row(far_sources, -1)[:, None] == at_leaf[None, :]
    same = row_part[:, None] == at_part[None, :]
    sign = jnp.where(row_part == 0, -1.0, 1.0)[:, None]
    pick_far = jnp.concatenate(
        [jnp.where(hit & same, 1.0, 0.0), jnp.where(hit & ~same, sign, 0.0)], 0
    ).astype(jnp.bfloat16)
    ranks = jnp.broadcast_to(by_row(far_ranks[0], 0)[:, None], (2 * slots, leaf))
    contrib = call(
        functools.partial(far_kernel, tasks), (2 * slots, leaf), jnp.bfloat16
    )(
        pick_far,
        gathered,
        ranks,
        far_right[0].reshape(tasks, 2 * leaf, leaf),
        far_left[0].reshape(tasks, 2 * leaf, leaf),
    )

    both_targets = lax.all_gather(far_targets, "core", axis=0, tiled=False)
    both_terms = lax.all_gather(contrib, "core", axis=0, tiled=True)
    goal = jnp.concatenate([by_row(both_targets[i], -1) for i in range(CORES)])
    out_row = jnp.arange(chips * 2 * leaves, dtype=jnp.int32)
    out_leaf = (out_row // (2 * leaves) * CORES + core) * leaves + out_row % leaves
    out_part = out_row // leaves % 2
    place = (out_leaf[:, None] == goal[None, :]) & (
        out_part[:, None] == jnp.tile(row_part, CORES)[None, :]
    )
    spread = dot(place.astype(jnp.bfloat16), both_terms).astype(jnp.bfloat16)
    arrived = lax.all_to_all(
        spread.reshape(chips, 2 * leaves, leaf), "chip", 0, 0, tiled=True
    )

    wanted = jnp.broadcast_to(near_leaves.T[:, None, :], (near, 2, leaves)).reshape(-1)
    wanted_part = jnp.arange(near * 2 * leaves, dtype=jnp.int32) // leaves % 2
    pick_near = (wanted[:, None] == at_leaf[None, :]) & (wanted_part[:, None] == at_part[None, :])
    near_field = call(near_kernel, (2 * leaves, leaf), jnp.float32)(
        pick_near.astype(jnp.bfloat16),
        gathered,
        near_blocks[0].reshape(leaves, near, 2 * leaf, leaf),
    )

    field = near_field + jnp.sum(arrived.astype(jnp.float32), 0)
    return field.reshape(1, 2, leaves * leaf).astype(jnp.bfloat16)


def solution(mesh):
    freq_groups, elem_groups = mesh.devices.shape
    split = Mesh(
        mesh.devices.reshape(freq_groups, elem_groups // CORES, CORES), ("freq", "chip", "core")
    )
    elem = ("chip", "core")
    in_specs = (
        P("freq", elem),
        P("freq", elem, None, None, None, None),
        P(elem, None),
        P("freq", elem, None, None, None),
        P("freq", elem, None, None, None),
        P("freq", elem),
        P(elem),
        P(elem),
    )
    out_specs = P("freq", None, elem)
    return jax.shard_map(
        per_device, mesh=split, in_specs=in_specs, out_specs=out_specs, check_vma=False
    )
```

```python
import functools
import math

import jax
import jax.numpy as jnp
from jax import lax
from jax.experimental import pallas as pl
from jax.experimental.pallas import tpu as pltpu
from jax.sharding import Mesh
from jax.sharding import PartitionSpec as P

fall_total = 0.25
CORES = 2
GROUP = 8
TILE = 2 * GROUP
LANES = 128
LIMIT = 32 * 1024 * 1024


def rotated(size):
    return [(i + size // 2) % size for i in range(size)]


def dot(first_op, second_op, transposed=False):
    dims = (((1,), (1 if transposed else 0,)), ((), ()))
    return lax.dot_general(first_op, second_op, dims, preferred_element_type=jnp.float32)


def iota(shape, dim):
    return lax.broadcasted_iota(jnp.int32, shape, dim)


def turn(direct, crossed):
    swapped = jnp.concatenate([-crossed[GROUP:], crossed[:GROUP]], 0)
    return direct + swapped


def chosen(where_at, values, fill):
    out = jnp.full(where_at.shape, fill, jnp.int32)
    for i, value in enumerate(values):
        out = jnp.where(where_at == i, value, out)
    return out


def leaf_codes(rows, chunk, chips):
    lane = iota((rows, LANES), 1)
    chunks_of_core = chips * TILE // LANES
    base = lane // TILE * (CORES * TILE) + lane % GROUP * 2 + lane // GROUP % 2
    return (
        base
        + chunk % chunks_of_core * (LANES * CORES)
        + chunk // chunks_of_core * TILE
    )


def partial_kernel(total_freq, total_steps, history_ref, out_ref, held, sem):
    copy = pltpu.make_async_copy(history_ref, held, sem)
    copy.start()
    steps = history_ref.shape[0]
    rows = 2 * total_freq
    leaf = out_ref.shape[-1]
    leaves = history_ref.shape[1] // leaf
    row = iota((rows, steps), 0)
    step = lax.axis_index("freq") * steps + iota((rows, steps), 1)
    freq = ((row >> 1) + total_freq // 2) % total_freq * (total_steps // total_freq) + 1
    phase = (freq * step + (row & 1) * (total_steps // 4)) & (total_steps - 1)
    angle = 2.0 * math.pi / total_steps * phase.astype(jnp.float32)
    damping = jnp.exp(step.astype(jnp.float32) * (math.log(fall_total) / total_steps))
    weights = (damping * jnp.cos(angle) / math.sqrt(total_steps)).astype(jnp.bfloat16)
    copy.wait()
    part = dot(weights, held[...])
    for l in range(leaves):
        out_ref[pl.ds(l, rows, stride=leaves), :] = part[:, l * leaf : (l + 1) * leaf]


def plan_kernel(chips, sources_ref, ranks_ref, targets_ref, pick_ref, depth_ref, goal_ref):
    tasks = sources_ref.shape[0]
    rows = depth_ref.shape[0]
    row = iota((rows, LANES), 0)
    row_task = row // TILE * GROUP + row % GROUP
    row_part = row // GROUP % 2
    source = chosen(row_task, [sources_ref[t] for t in range(tasks)], -1)
    depth_ref[...] = chosen(row_task, [ranks_ref[t] for t in range(tasks)], 0)
    same = source * 2 + row_part
    other = source * 2 + 1 - row_part
    sign = jnp.where(row_part == 0, -1.0, 1.0)
    for chunk in range(pick_ref.shape[1] // LANES):
        codes = leaf_codes(rows, chunk, chips)
        lanes = slice(chunk * LANES, (chunk + 1) * LANES)
        pick_ref[:rows, lanes] = jnp.where(same == codes, 1.0, 0.0).astype(jnp.bfloat16)
        pick_ref[rows:, lanes] = jnp.where(other == codes, sign, 0.0).astype(jnp.bfloat16)
    lane = iota((rows, LANES), 1) % rows
    lane_task = lane // TILE * GROUP + lane % GROUP
    target = chosen(lane_task, [targets_ref[t] for t in range(tasks)], -1)
    spare = tasks // GROUP * TILE + tasks % GROUP
    goal_ref[...] = jnp.where(
        row == spare, target >> 3, jnp.where(row == spare + 1, target & 7, 0)
    ).astype(jnp.float32)


def far_kernel(tasks, pick_ref, depth_ref, goal_ref, gathered_ref, right_ref, left_ref, out_ref):
    picked = dot(pick_ref[...], gathered_ref[...]).astype(jnp.bfloat16)
    half = picked.shape[0] // 2
    pair = jnp.concatenate([picked[:half], picked[half:]], 1)
    leaf = left_ref.shape[-1]
    own = iota((TILE, leaf), 0) % GROUP
    lane = iota((TILE, leaf), 1)
    for start in range(0, tasks, GROUP):
        rows = slice(2 * start, 2 * start + TILE)
        here = range(start, min(start + GROUP, tasks))
        coeff = jnp.zeros((TILE, leaf), jnp.float32)
        for t in here:
            coeff = jnp.where(own == t - start, dot(pair[rows], right_ref[t]), coeff)
        coeff = jnp.where(lane < depth_ref[rows, :], coeff, 0.0).astype(jnp.bfloat16)
        direct = jnp.zeros((TILE, leaf), jnp.float32)
        crossed = jnp.zeros((TILE, leaf), jnp.float32)
        for t in here:
            both = dot(coeff, left_ref[t], True)
            direct = jnp.where(own == t - start, both[:, :leaf], direct)
            crossed = jnp.where(own == t - start, both[:, leaf:], crossed)
        terms = turn(direct, crossed) + goal_ref[rows, :]
        out_ref[rows, :] = terms.astype(jnp.bfloat16)


def scatter_kernel(tasks, chips, terms_ref, out_ref):
    terms = terms_ref[...]
    columns = terms.shape[0]
    rows = columns // CORES
    spare = tasks // GROUP * TILE + tasks % GROUP
    lane = iota((1, terms.shape[1]), 1)
    wide = terms.astype(jnp.float32)

    def along(at):
        return jnp.where(lane < rows, wide[at : at + 1], wide[rows + at : rows + at + 1])

    goal = (along(spare) * GROUP + along(spare + 1)).astype(jnp.int32)
    code = (goal * 2 + lane // GROUP % 2)[:, :columns]
    row = iota((TILE, columns), 0)
    base = (lax.axis_index("core") * GROUP + row % GROUP) * 2 + row // GROUP
    place = jnp.concatenate(
        [jnp.where(code - chip * (CORES * TILE) == base, 1.0, 0.0) for chip in range(chips)], 0
    )
    out_ref[...] = dot(place.astype(jnp.bfloat16), terms).astype(jnp.bfloat16)


def near_kernel(chips, leaves_ref, gathered_ref, blocks_ref, out_ref):
    leaves, near = blocks_ref.shape[:2]
    leaf = blocks_ref.shape[-1]
    own = iota((TILE, leaf), 0) % GROUP
    part = iota((TILE, leaf), 0) // GROUP
    wanted = jnp.concatenate(
        [chosen(own, [leaves_ref[l, n] for l in range(leaves)], -1) * 2 + part for n in range(near)],
        0,
    )
    pick = jnp.concatenate(
        [
            jnp.where(wanted == leaf_codes(near * TILE, chunk, chips), 1.0, 0.0)
            for chunk in range(gathered_ref.shape[0] // LANES)
        ],
        1,
    )
    picked = dot(pick.astype(jnp.bfloat16), gathered_ref[...]).astype(jnp.bfloat16)
    direct = jnp.zeros((TILE, leaf), jnp.float32)
    crossed = jnp.zeros((TILE, leaf), jnp.float32)
    for n in range(near):
        view = picked[TILE * n : TILE * (n + 1)]
        for l in range(leaves):
            both = dot(view, blocks_ref[l, n], True)
            direct = direct + jnp.where(own == l, both[:, :leaf], 0.0)
            crossed = crossed + jnp.where(own == l, both[:, leaf:], 0.0)
    out_ref[...] = turn(direct, crossed)


def call(kernel, outs, spaces, scratch=()):
    return pl.pallas_call(
        kernel,
        out_shape=[jax.ShapeDtypeStruct(shape, dtype) for shape, dtype in outs],
        in_specs=[pl.BlockSpec(memory_space=space) for space in spaces],
        out_specs=[pl.BlockSpec(memory_space=pltpu.VMEM) for _ in outs],
        scratch_shapes=scratch,
        compiler_params=pltpu.CompilerParams(vmem_limit_bytes=LIMIT),
    )


def per_device(
    history, near_blocks, near_leaves, far_left, far_right, far_ranks, far_targets, far_sources
):
    vmem, smem = pltpu.VMEM, pltpu.SMEM
    freq_groups = lax.axis_size("freq")
    chips = lax.axis_size("chip")
    total_freq = far_ranks.shape[0] * freq_groups
    total_steps = history.shape[0] * freq_groups
    leaf = near_blocks.shape[-1]
    leaves = near_blocks.shape[1]
    near = near_blocks.shape[2]
    tasks = far_ranks.shape[1]
    slots = -(-tasks // GROUP) * GROUP

    (partial,) = call(
        functools.partial(partial_kernel, total_freq, total_steps),
        [((total_freq * TILE, leaf), jnp.float32)],
        [pltpu.HBM],
        [pltpu.VMEM(history.shape, history.dtype), pltpu.SemaphoreType.DMA],
    )(history)
    shares = lax.all_to_all(
        partial.reshape(total_freq, TILE, leaf),
        "freq",
        0,
        0,
        axis_index_groups=[rotated(freq_groups)],
        tiled=True,
    )
    spectrum = jnp.sum(shares, 0).astype(jnp.bfloat16)
    copies = jnp.broadcast_to(spectrum[None], (chips,) + spectrum.shape)
    same_core = lax.all_to_all(copies, "chip", 0, 0, tiled=True)
    gathered = lax.all_gather(same_core, "core", axis=0, tiled=False)
    gathered = gathered.reshape(CORES * chips * TILE, leaf)

    pick, depth, goal = call(
        functools.partial(plan_kernel, chips),
        [
            ((4 * slots, gathered.shape[0]), jnp.bfloat16),
            ((2 * slots, leaf), jnp.int32),
            ((2 * slots, leaf), jnp.float32),
        ],
        [smem, smem, smem],
    )(far_sources, far_ranks[0], far_targets)
    (terms,) = call(
        functools.partial(far_kernel, tasks),
        [((2 * slots, leaf), jnp.bfloat16)],
        [vmem] * 6,
    )(
        pick,
        depth,
        goal,
        gathered,
        far_right[0].reshape(tasks, 2 * leaf, leaf),
        far_left[0].reshape(tasks, 2 * leaf, leaf),
    )

    both_terms = lax.all_gather(terms, "core", axis=0, tiled=True)
    (spread,) = call(
        functools.partial(scatter_kernel, tasks, chips),
        [((chips * TILE, leaf), jnp.bfloat16)],
        [vmem],
    )(both_terms)
    arrived = lax.all_to_all(spread.reshape(chips, TILE, leaf), "chip", 0, 0, tiled=True)

    (near_field,) = call(
        functools.partial(near_kernel, chips),
        [((TILE, leaf), jnp.float32)],
        [smem, vmem, vmem],
    )(near_leaves, gathered, near_blocks[0].reshape(leaves, near, 2 * leaf, leaf))

    field = near_field + jnp.sum(arrived.astype(jnp.float32), 0)
    return field.reshape(1, 2, leaves * leaf).astype(jnp.bfloat16)


def solution(mesh):
    freq_groups, elem_groups = mesh.devices.shape
    split = Mesh(
        mesh.devices.reshape(freq_groups, elem_groups // CORES, CORES), ("freq", "chip", "core")
    )
    elem = ("chip", "core")
    in_specs = (
        P("freq", elem),
        P("freq", elem, None, None, None, None),
        P(elem, None),
        P("freq", elem, None, None, None),
        P("freq", elem, None, None, None),
        P("freq", elem),
        P(elem),
        P(elem),
    )
    out_specs = P("freq", None, elem)
    return jax.shard_map(
        per_device, mesh=split, in_specs=in_specs, out_specs=out_specs, check_vma=False
    )
```

```python
import functools
import math

import jax
import jax.numpy as jnp
from jax import lax
from jax.experimental import pallas as pl
from jax.experimental.pallas import tpu as pltpu
from jax.sharding import Mesh
from jax.sharding import PartitionSpec as P

fall_total = 0.25
CORES = 2
GROUP = 8
TILE = 2 * GROUP
LANES = 128
LIMIT = 32 * 1024 * 1024


def rotated(size, first):
    return [(i + first) % size for i in range(size)]


def last(size):
    return size - 1


def dot(first_op, second_op, transposed=False):
    dims = (((1,), (1 if transposed else 0,)), ((), ()))
    return lax.dot_general(first_op, second_op, dims, preferred_element_type=jnp.float32)


def iota(shape, dim):
    return lax.broadcasted_iota(jnp.int32, shape, dim)


def turn(direct, crossed):
    swapped = jnp.concatenate([-crossed[GROUP:], crossed[:GROUP]], 0)
    return direct + swapped


def chosen(where_at, values, fill):
    out = jnp.full(where_at.shape, fill, jnp.int32)
    for i, value in enumerate(values):
        out = jnp.where(where_at == i, value, out)
    return out


def leaf_codes(chunk, chips):
    at = chunk * LANES + iota((1, LANES), 1)
    core = at // (chips * TILE)
    chip = (at // TILE + last(chips)) % chips
    return (chip * CORES + core) * TILE + at % GROUP * 2 + at // GROUP % 2


def partial_kernel(total_freq, total_steps, history_ref, out_ref, held, sem):
    copy = pltpu.make_async_copy(history_ref, held, sem)
    copy.start()
    steps = history_ref.shape[0]
    rows = 2 * total_freq
    leaf = out_ref.shape[-1]
    leaves = history_ref.shape[1] // leaf
    row = iota((rows, steps), 0)
    step = lax.axis_index("freq") * steps + iota((rows, steps), 1)
    freq = ((row >> 1) + total_freq // 2) % total_freq * (total_steps // total_freq) + 1
    phase = (freq * step + (row & 1) * (total_steps // 4)) & (total_steps - 1)
    angle = 2.0 * math.pi / total_steps * phase.astype(jnp.float32)
    damping = jnp.exp(step.astype(jnp.float32) * (math.log(fall_total) / total_steps))
    weights = (damping * jnp.cos(angle) / math.sqrt(total_steps)).astype(jnp.bfloat16)
    copy.wait()
    part = dot(weights, held[...])
    for l in range(leaves):
        out_ref[pl.ds(l, rows, stride=leaves), :] = part[:, l * leaf : (l + 1) * leaf]


def plan_kernel(
    chips,
    sources_ref,
    ranks_ref,
    targets_ref,
    right_ref,
    left_ref,
    pick_ref,
    depth_ref,
    goal_ref,
):
    tasks = sources_ref.shape[0]
    rows = depth_ref.shape[0]
    row = iota((rows, LANES), 0)
    row_task = row // TILE * GROUP + row % GROUP
    row_part = row // GROUP % 2
    source = chosen(row_task, [sources_ref[t] for t in range(tasks)], -1)
    depth_ref[...] = chosen(row_task, [ranks_ref[t] for t in range(tasks)], 0)
    same = source * 2 + row_part
    other = source * 2 + 1 - row_part
    sign = jnp.where(row_part == 0, -1.0, 1.0)
    for chunk in range(pick_ref.shape[1] // LANES):
        codes = leaf_codes(chunk, chips)
        lanes = slice(chunk * LANES, (chunk + 1) * LANES)
        pick_ref[:rows, lanes] = jnp.where(same == codes, 1.0, 0.0).astype(jnp.bfloat16)
        pick_ref[rows:, lanes] = jnp.where(other == codes, sign, 0.0).astype(jnp.bfloat16)
    lane = iota((rows, LANES), 1) % rows
    lane_task = lane // TILE * GROUP + lane % GROUP
    target = chosen(lane_task, [targets_ref[t] for t in range(tasks)], -1)
    spare = tasks // GROUP * TILE + tasks % GROUP
    goal_ref[...] = jnp.where(
        row == spare, target >> 3, jnp.where(row == spare + 1, target & 7, 0)
    ).astype(jnp.float32)


def far_kernel(tasks, pick_ref, depth_ref, goal_ref, gathered_ref, right_ref, left_ref, out_ref):
    picked = dot(pick_ref[...], gathered_ref[...]).astype(jnp.bfloat16)
    half = picked.shape[0] // 2
    pair = jnp.concatenate([picked[:half], picked[half:]], 1)
    leaf = left_ref.shape[-1]
    own = iota((TILE, leaf), 0) % GROUP
    lane = iota((TILE, leaf), 1)
    for start in range(0, tasks, GROUP):
        rows = slice(2 * start, 2 * start + TILE)
        here = range(start, min(start + GROUP, tasks))
        coeff = jnp.zeros((TILE, leaf), jnp.float32)
        for t in here:
            coeff = jnp.where(own == t - start, dot(pair[rows], right_ref[t]), coeff)
        coeff = jnp.where(lane < depth_ref[rows, :], coeff, 0.0).astype(jnp.bfloat16)
        direct = jnp.zeros((TILE, leaf), jnp.float32)
        crossed = jnp.zeros((TILE, leaf), jnp.float32)
        for t in here:
            both = dot(coeff, left_ref[t], True)
            direct = jnp.where(own == t - start, both[:, :leaf], direct)
            crossed = jnp.where(own == t - start, both[:, leaf:], crossed)
        terms = turn(direct, crossed) + goal_ref[rows, :]
        out_ref[rows, :] = terms.astype(jnp.bfloat16)


def scatter_kernel(tasks, chips, terms_ref, out_ref):
    terms = terms_ref[...]
    columns = terms.shape[0]
    rows = columns // CORES
    spare = tasks // GROUP * TILE + tasks % GROUP
    lane = iota((1, terms.shape[1]), 1)
    wide = terms.astype(jnp.float32)

    def along(at):
        return jnp.where(lane < rows, wide[at : at + 1], wide[rows + at : rows + at + 1])

    goal = (along(spare) * GROUP + along(spare + 1)).astype(jnp.int32)
    code = (goal * 2 + lane // GROUP % 2)[:, :columns]
    row = iota((TILE, columns), 0)
    base = (lax.axis_index("core") * GROUP + row % GROUP) * 2 + row // GROUP
    place = jnp.concatenate(
        [jnp.where(code - chip * (CORES * TILE) == base, 1.0, 0.0) for chip in range(chips)], 0
    )
    out_ref[...] = dot(place.astype(jnp.bfloat16), terms).astype(jnp.bfloat16)


def near_kernel(chips, leaves_ref, gathered_ref, blocks_ref, out_ref):
    leaves, near = blocks_ref.shape[:2]
    leaf = blocks_ref.shape[-1]
    own = iota((TILE, leaf), 0) % GROUP
    part = iota((TILE, leaf), 0) // GROUP
    wanted = jnp.concatenate(
        [chosen(own, [leaves_ref[l, n] for l in range(leaves)], -1) * 2 + part for n in range(near)],
        0,
    )
    pick = jnp.concatenate(
        [
            jnp.where(wanted == leaf_codes(chunk, chips), 1.0, 0.0)
            for chunk in range(gathered_ref.shape[0] // LANES)
        ],
        1,
    )
    picked = dot(pick.astype(jnp.bfloat16), gathered_ref[...]).astype(jnp.bfloat16)
    direct = jnp.zeros((TILE, leaf), jnp.float32)
    crossed = jnp.zeros((TILE, leaf), jnp.float32)
    for n in range(near):
        view = picked[TILE * n : TILE * (n + 1)]
        for l in range(leaves):
            both = dot(view, blocks_ref[l, n], True)
            direct = direct + jnp.where(own == l, both[:, :leaf], 0.0)
            crossed = crossed + jnp.where(own == l, both[:, leaf:], 0.0)
    out_ref[...] = turn(direct, crossed)


def call(kernel, outs, spaces, scratch=()):
    return pl.pallas_call(
        kernel,
        out_shape=[jax.ShapeDtypeStruct(shape, dtype) for shape, dtype in outs],
        in_specs=[pl.BlockSpec(memory_space=space) for space in spaces],
        out_specs=[pl.BlockSpec(memory_space=pltpu.VMEM) for _ in outs],
        scratch_shapes=scratch,
        compiler_params=pltpu.CompilerParams(vmem_limit_bytes=LIMIT),
    )


def per_device(
    history, near_blocks, near_leaves, far_left, far_right, far_ranks, far_targets, far_sources
):
    vmem, smem = pltpu.VMEM, pltpu.SMEM
    freq_groups = lax.axis_size("freq")
    chips = lax.axis_size("chip")
    total_freq = far_ranks.shape[0] * freq_groups
    total_steps = history.shape[0] * freq_groups
    leaf = near_blocks.shape[-1]
    leaves = near_blocks.shape[1]
    near = near_blocks.shape[2]
    tasks = far_ranks.shape[1]
    slots = -(-tasks // GROUP) * GROUP

    (partial,) = call(
        functools.partial(partial_kernel, total_freq, total_steps),
        [((total_freq * TILE, leaf), jnp.float32)],
        [pltpu.HBM],
        [pltpu.VMEM(history.shape, history.dtype), pltpu.SemaphoreType.DMA],
    )(history)
    shares = lax.all_to_all(
        partial.reshape(total_freq, TILE, leaf),
        "freq",
        0,
        0,
        axis_index_groups=[rotated(freq_groups, freq_groups // 2)],
        tiled=True,
    )
    spectrum = jnp.sum(shares, 0).astype(jnp.bfloat16)
    copies = jnp.broadcast_to(spectrum[None], (chips,) + spectrum.shape)
    same_core = lax.all_to_all(
        copies, "chip", 0, 0, axis_index_groups=[rotated(chips, last(chips))], tiled=True
    )
    gathered = lax.all_gather(same_core, "core", axis=0, tiled=False)
    gathered = gathered.reshape(CORES * chips * TILE, leaf)

    right = far_right[0].reshape(tasks, 2 * leaf, leaf)
    left = far_left[0].reshape(tasks, 2 * leaf, leaf)
    pick, depth, goal = call(
        functools.partial(plan_kernel, chips),
        [
            ((4 * slots, gathered.shape[0]), jnp.bfloat16),
            ((2 * slots, leaf), jnp.int32),
            ((2 * slots, leaf), jnp.float32),
        ],
        [smem, smem, smem, vmem, vmem],
    )(far_sources, far_ranks[0], far_targets, right, left)
    (terms,) = call(
        functools.partial(far_kernel, tasks),
        [((2 * slots, leaf), jnp.bfloat16)],
        [vmem] * 6,
    )(
        pick,
        depth,
        goal,
        gathered,
        right,
        left,
    )

    both_terms = lax.all_gather(terms, "core", axis=0, tiled=True)
    (spread,) = call(
        functools.partial(scatter_kernel, tasks, chips),
        [((chips * TILE, leaf), jnp.bfloat16)],
        [vmem],
    )(both_terms)
    arrived = lax.all_to_all(spread.reshape(chips, TILE, leaf), "chip", 0, 0, tiled=True)

    (near_field,) = call(
        functools.partial(near_kernel, chips),
        [((TILE, leaf), jnp.float32)],
        [smem, vmem, vmem],
    )(near_leaves, gathered, near_blocks[0].reshape(leaves, near, 2 * leaf, leaf))

    field = near_field + jnp.sum(arrived.astype(jnp.float32), 0)
    return field.reshape(1, 2, leaves * leaf).astype(jnp.bfloat16)


def solution(mesh):
    freq_groups, elem_groups = mesh.devices.shape
    split = Mesh(
        mesh.devices.reshape(freq_groups, elem_groups // CORES, CORES), ("freq", "chip", "core")
    )
    elem = ("chip", "core")
    in_specs = (
        P("freq", elem),
        P("freq", elem, None, None, None, None),
        P(elem, None),
        P("freq", elem, None, None, None),
        P("freq", elem, None, None, None),
        P("freq", elem),
        P(elem),
        P(elem),
    )
    out_specs = P("freq", None, elem)
    return jax.shard_map(
        per_device, mesh=split, in_specs=in_specs, out_specs=out_specs, check_vma=False
    )
```

```python
import functools
import math

import jax
import jax.numpy as jnp
from jax import lax
from jax.experimental import pallas as pl
from jax.experimental.pallas import tpu as pltpu
from jax.sharding import Mesh
from jax.sharding import PartitionSpec as P

fall_total = 0.25
CORES = 2
GROUP = 8
TILE = 2 * GROUP
LANES = 128
LIMIT = 16 * 1024 * 1024


def rotated(size, first):
    return [(i + first) % size for i in range(size)]


def first_chip(chips):
    return chips * 3 // 4 + 2


def dot(first_op, second_op, transposed=False):
    dims = (((1,), (1 if transposed else 0,)), ((), ()))
    return lax.dot_general(first_op, second_op, dims, preferred_element_type=jnp.float32)


def iota(shape, dim):
    return lax.broadcasted_iota(jnp.int32, shape, dim)


def turn(direct, crossed):
    swapped = jnp.concatenate([-crossed[GROUP:], crossed[:GROUP]], 0)
    return direct + swapped


def chosen(where_at, values, fill):
    out = jnp.full(where_at.shape, fill, jnp.int32)
    for i, value in enumerate(values):
        out = jnp.where(where_at == i, value, out)
    return out


def leaf_codes(chunk, chips):
    at = chunk * LANES + iota((1, LANES), 1)
    core = at // (chips * TILE)
    chip = (at // TILE + first_chip(chips)) % chips
    return (chip * CORES + core) * TILE + at % GROUP * 2 + at // GROUP % 2


def partial_kernel(total_freq, total_steps, history_ref, out_ref, held, sem):
    copy = pltpu.make_async_copy(history_ref, held, sem)
    copy.start()
    steps = history_ref.shape[0]
    rows = 2 * total_freq
    leaf = out_ref.shape[-1]
    leaves = history_ref.shape[1] // leaf
    row = iota((rows, steps), 0)
    step = lax.axis_index("freq") * steps + iota((rows, steps), 1)
    freq = ((row >> 1) + total_freq // 2) % total_freq * (total_steps // total_freq) + 1
    phase = (freq * step + (row & 1) * (total_steps // 4)) & (total_steps - 1)
    angle = 2.0 * math.pi / total_steps * phase.astype(jnp.float32)
    damping = jnp.exp(step.astype(jnp.float32) * (math.log(fall_total) / total_steps))
    weights = (damping * jnp.cos(angle) / math.sqrt(total_steps)).astype(jnp.bfloat16)
    copy.wait()
    part = dot(weights, held[...])
    for l in range(leaves):
        out_ref[pl.ds(l, rows, stride=leaves), :] = part[:, l * leaf : (l + 1) * leaf]


def plan_kernel(chips, tasks, index_ref, left_ref, pick_ref, held_ref, sem):
    copy = pltpu.make_async_copy(left_ref, held_ref, sem)
    copy.start()
    rows = pick_ref.shape[0] // 2
    row = iota((rows, LANES), 0)
    lane = iota((rows, LANES), 1)
    row_part = row // GROUP % 2
    own = lane == row // TILE * GROUP + row % GROUP
    index = index_ref[...].astype(jnp.float32)

    def by_row(at):
        return jnp.sum(jnp.where(own, index[at : at + 1], 0.0), 1, keepdims=True)

    source = by_row(0).astype(jnp.int32)
    same = source * 2 + row_part
    other = source * 2 + 1 - row_part
    sign = jnp.where(row_part == 0, -1.0, 1.0)
    chunks = pick_ref.shape[1] // LANES - 1
    for chunk in range(chunks):
        codes = leaf_codes(chunk, chips)
        lanes = slice(chunk * LANES, (chunk + 1) * LANES)
        pick_ref[:rows, lanes] = jnp.where(same == codes, 1.0, 0.0).astype(jnp.bfloat16)
        pick_ref[rows:, lanes] = jnp.where(other == codes, sign, 0.0).astype(jnp.bfloat16)
    extra = slice(chunks * LANES, (chunks + 1) * LANES)
    pick_ref[:rows, extra] = jnp.broadcast_to(by_row(1), (rows, LANES)).astype(jnp.bfloat16)
    target = jnp.sum(jnp.where(row == lane % rows, by_row(2), 0.0), 0, keepdims=True)
    target = target.astype(jnp.int32)
    spare = tasks // GROUP * TILE + tasks % GROUP
    goal = jnp.where(row == spare, target >> 3, jnp.where(row == spare + 1, target & 7, 0))
    pick_ref[rows:, extra] = goal.astype(jnp.float32).astype(jnp.bfloat16)
    copy.wait()


def far_kernel(tasks, pick_ref, gathered_ref, right_ref, left_ref, out_ref):
    columns = gathered_ref.shape[0]
    picked = dot(pick_ref[:, :columns], gathered_ref[...]).astype(jnp.bfloat16)
    extra = pick_ref[:, columns:].astype(jnp.float32)
    half = picked.shape[0] // 2
    pair = jnp.concatenate([picked[:half], picked[half:]], 1)
    leaf = left_ref.shape[-1]
    own = iota((TILE, leaf), 0) % GROUP
    lane = iota((TILE, leaf), 1).astype(jnp.float32)
    for start in range(0, tasks, GROUP):
        rows = slice(2 * start, 2 * start + TILE)
        here = range(start, min(start + GROUP, tasks))
        coeff = jnp.zeros((TILE, leaf), jnp.float32)
        for t in here:
            coeff = jnp.where(own == t - start, dot(pair[rows], right_ref[t]), coeff)
        coeff = jnp.where(lane < extra[rows], coeff, 0.0).astype(jnp.bfloat16)
        direct = jnp.zeros((TILE, leaf), jnp.float32)
        crossed = jnp.zeros((TILE, leaf), jnp.float32)
        for t in here:
            both = dot(coeff, left_ref[t], True)
            direct = jnp.where(own == t - start, both[:, :leaf], direct)
            crossed = jnp.where(own == t - start, both[:, leaf:], crossed)
        goal = extra[half + 2 * start : half + 2 * start + TILE]
        terms = turn(direct, crossed) + goal
        out_ref[rows, :] = terms.astype(jnp.bfloat16)


def scatter_kernel(tasks, chips, terms_ref, out_ref):
    terms = terms_ref[...]
    columns = terms.shape[0]
    rows = columns // CORES
    spare = tasks // GROUP * TILE + tasks % GROUP
    lane = iota((1, terms.shape[1]), 1)
    wide = terms.astype(jnp.float32)

    def along(at):
        return jnp.where(lane < rows, wide[at : at + 1], wide[rows + at : rows + at + 1])

    goal = (along(spare) * GROUP + along(spare + 1)).astype(jnp.int32)
    code = (goal * 2 + lane // GROUP % 2)[:, :columns]
    row = iota((TILE, columns), 0)
    base = (lax.axis_index("core") * GROUP + row % GROUP) * 2 + row // GROUP
    place = jnp.concatenate(
        [
            jnp.where(code - chip * (CORES * TILE) == base, 1.0, 0.0)
            for chip in rotated(chips, first_chip(chips))
        ],
        0,
    )
    out_ref[...] = dot(place.astype(jnp.bfloat16), terms).astype(jnp.bfloat16)


def near_kernel(chips, leaves_ref, gathered_ref, blocks_ref, out_ref):
    leaves, near = blocks_ref.shape[:2]
    leaf = blocks_ref.shape[-1]
    own = iota((TILE, leaf), 0) % GROUP
    part = iota((TILE, leaf), 0) // GROUP
    wanted = jnp.concatenate(
        [chosen(own, [leaves_ref[l, n] for l in range(leaves)], -1) * 2 + part for n in range(near)],
        0,
    )
    pick = jnp.concatenate(
        [
            jnp.where(wanted == leaf_codes(chunk, chips), 1.0, 0.0)
            for chunk in range(gathered_ref.shape[0] // LANES)
        ],
        1,
    )
    picked = dot(pick.astype(jnp.bfloat16), gathered_ref[...]).astype(jnp.bfloat16)
    direct = jnp.zeros((TILE, leaf), jnp.float32)
    crossed = jnp.zeros((TILE, leaf), jnp.float32)
    for n in range(near):
        view = picked[TILE * n : TILE * (n + 1)]
        for l in range(leaves):
            both = dot(view, blocks_ref[l, n], True)
            direct = direct + jnp.where(own == l, both[:, :leaf], 0.0)
            crossed = crossed + jnp.where(own == l, both[:, leaf:], 0.0)
    out_ref[...] = turn(direct, crossed)


def call(kernel, outs, spaces, scratch=(), hide=2):
    return pl.pallas_call(
        kernel,
        out_shape=[jax.ShapeDtypeStruct(shape, dtype) for shape, dtype in outs],
        in_specs=[pl.BlockSpec(memory_space=space) for space in spaces],
        out_specs=[pl.BlockSpec(memory_space=pltpu.VMEM) for _ in outs],
        scratch_shapes=scratch,
        cost_estimate=pl.CostEstimate(
            flops=0, transcendentals=0, bytes_accessed=hide * 1024 * 1024
        ),
        compiler_params=pltpu.CompilerParams(vmem_limit_bytes=LIMIT),
    )


def per_device(
    history, near_blocks, near_leaves, far_left, far_right, far_ranks, far_targets, far_sources
):
    vmem, smem = pltpu.VMEM, pltpu.SMEM
    freq_groups = lax.axis_size("freq")
    chips = lax.axis_size("chip")
    total_freq = far_ranks.shape[0] * freq_groups
    total_steps = history.shape[0] * freq_groups
    leaf = near_blocks.shape[-1]
    leaves = near_blocks.shape[1]
    near = near_blocks.shape[2]
    tasks = far_ranks.shape[1]
    slots = -(-tasks // GROUP) * GROUP

    (partial,) = call(
        functools.partial(partial_kernel, total_freq, total_steps),
        [((total_freq * TILE, leaf), jnp.float32)],
        [pltpu.HBM],
        [pltpu.VMEM(history.shape, history.dtype), pltpu.SemaphoreType.DMA],
    )(history)
    shares = lax.all_to_all(
        partial.reshape(total_freq, TILE, leaf),
        "freq",
        0,
        0,
        axis_index_groups=[rotated(freq_groups, freq_groups // 2)],
        tiled=True,
    )
    spectrum = jnp.sum(shares, 0).astype(jnp.bfloat16)
    copies = jnp.broadcast_to(spectrum[None], (chips,) + spectrum.shape)
    same_core = lax.all_to_all(
        copies, "chip", 0, 0, axis_index_groups=[rotated(chips, first_chip(chips))], tiled=True
    )
    gathered = lax.all_gather(same_core, "core", axis=0, tiled=False)
    gathered = gathered.reshape(CORES * chips * TILE, leaf)

    index = jnp.stack([far_sources, far_ranks[0], far_targets])
    index = jnp.pad(index, ((0, GROUP - index.shape[0]), (0, LANES - tasks)), constant_values=-1)
    left = far_left[0].reshape(tasks, 2 * leaf, leaf)
    pick, left = call(
        functools.partial(plan_kernel, chips, tasks),
        [
            ((4 * slots, gathered.shape[0] + LANES), jnp.bfloat16),
            (left.shape, left.dtype),
        ],
        [vmem, pl.ANY],
        [pltpu.SemaphoreType.DMA],
        hide=8,
    )(index, left)
    (terms,) = call(
        functools.partial(far_kernel, tasks),
        [((2 * slots, leaf), jnp.bfloat16)],
        [vmem] * 4,
    )(
        pick,
        gathered,
        far_right[0].reshape(tasks, 2 * leaf, leaf),
        left,
    )

    both_terms = lax.all_gather(terms, "core", axis=0, tiled=True)
    (spread,) = call(
        functools.partial(scatter_kernel, tasks, chips),
        [((chips * TILE, leaf), jnp.bfloat16)],
        [vmem],
    )(both_terms)
    arrived = lax.all_to_all(
        spread.reshape(chips, TILE, leaf),
        "chip",
        0,
        0,
        axis_index_groups=[rotated(chips, first_chip(chips))],
        tiled=True,
    )

    (near_field,) = call(
        functools.partial(near_kernel, chips),
        [((TILE, leaf), jnp.float32)],
        [smem, vmem, vmem],
    )(near_leaves, gathered, near_blocks[0].reshape(leaves, near, 2 * leaf, leaf))

    field = near_field + jnp.sum(arrived.astype(jnp.float32), 0)
    return field.reshape(1, 2, leaves * leaf).astype(jnp.bfloat16)


def solution(mesh):
    freq_groups, elem_groups = mesh.devices.shape
    split = Mesh(
        mesh.devices.reshape(freq_groups, elem_groups // CORES, CORES), ("freq", "chip", "core")
    )
    elem = ("chip", "core")
    in_specs = (
        P("freq", elem),
        P("freq", elem, None, None, None, None),
        P(elem, None),
        P("freq", elem, None, None, None),
        P("freq", elem, None, None, None),
        P("freq", elem),
        P(elem),
        P(elem),
    )
    out_specs = P("freq", None, elem)
    return jax.shard_map(
        per_device, mesh=split, in_specs=in_specs, out_specs=out_specs, check_vma=False
    )
```

```python
import functools
import math

import jax
import jax.numpy as jnp
from jax import lax
from jax.experimental import pallas as pl
from jax.experimental.pallas import tpu as pltpu
from jax.sharding import Mesh
from jax.sharding import PartitionSpec as P

fall_total = 0.25
CORES = 2
GROUP = 8
TILE = 2 * GROUP
LANES = 128


def rotated(size, first):
    return [(i + first) % size for i in range(size)]


def first_chip(chips):
    return chips * 3 // 4 + 2


def dot(first_op, second_op, transposed=False):
    dims = (((1,), (1 if transposed else 0,)), ((), ()))
    return lax.dot_general(first_op, second_op, dims, preferred_element_type=jnp.float32)


def iota(shape, dim):
    return lax.broadcasted_iota(jnp.int32, shape, dim)


def turn(direct, crossed):
    swapped = jnp.concatenate([-crossed[GROUP:], crossed[:GROUP]], 0)
    return direct + swapped


def chosen(where_at, values, fill):
    out = jnp.full(where_at.shape, fill, jnp.int32)
    for i, value in enumerate(values):
        out = jnp.where(where_at == i, value, out)
    return out


def leaf_codes(chunk, chips):
    at = chunk * LANES + iota((1, LANES), 1)
    core = at // (chips * TILE)
    chip = (at // TILE + first_chip(chips)) % chips
    return (chip * CORES + core) * TILE + at % GROUP * 2 + at // GROUP % 2


def plan(chips, pick_ref, sources_ref, ranks_ref, targets_ref, leaves_ref):
    tasks = sources_ref.shape[1]
    near, leaves = leaves_ref.shape
    rows = 2 * (-(-tasks // GROUP) * GROUP)
    row = iota((rows, LANES), 0)
    lane = iota((rows, LANES), 1)
    task = row // TILE * GROUP + row % GROUP
    part = row // GROUP % 2

    def by_row(ref):
        value = ref[...].astype(jnp.float32)
        found = jnp.where(iota((rows, tasks), 1) == task[:, :tasks], value, 0.0)
        return jnp.where(task < tasks, jnp.sum(found, 1, keepdims=True), -1.0)

    source = by_row(sources_ref).astype(jnp.int32)
    wanted = leaves_ref[...].astype(jnp.float32)
    own = iota((TILE, leaves), 1) == iota((TILE, leaves), 0) % GROUP
    listed = [
        jnp.sum(jnp.where(own, wanted[n : n + 1], 0.0), 1, keepdims=True) for n in range(near)
    ]
    near_part = iota((TILE, LANES), 0) // GROUP
    near_codes = [leaf.astype(jnp.int32) * 2 + near_part for leaf in listed]
    direct = source * 2 + part
    turned = source * 2 + 1 - part
    sign = jnp.where(part == 0, -1.0, 1.0)
    chunks = pick_ref.shape[1] // LANES - 1
    for chunk in range(chunks):
        codes = leaf_codes(chunk, chips)
        lanes = slice(chunk * LANES, (chunk + 1) * LANES)
        pick_ref[:rows, lanes] = jnp.where(direct == codes, 1.0, 0.0).astype(jnp.bfloat16)
        pick_ref[rows : 2 * rows, lanes] = jnp.where(turned == codes, sign, 0.0).astype(
            jnp.bfloat16
        )
        for n in range(near):
            pick_ref[2 * rows + n * TILE : 2 * rows + (n + 1) * TILE, lanes] = jnp.where(
                near_codes[n] == codes, 1.0, 0.0
            ).astype(jnp.bfloat16)
    extra = slice(chunks * LANES, (chunks + 1) * LANES)
    pick_ref[:rows, extra] = by_row(ranks_ref).astype(jnp.bfloat16)
    target = jnp.sum(jnp.where(row == lane % rows, by_row(targets_ref), 0.0), 0, keepdims=True)
    target = target.astype(jnp.int32)
    spare = tasks // GROUP * TILE + tasks % GROUP
    goal = jnp.where(row == spare, target >> 3, jnp.where(row == spare + 1, target & 7, 0))
    pick_ref[rows : 2 * rows, extra] = goal.astype(jnp.float32).astype(jnp.bfloat16)
    pick_ref[2 * rows :, extra] = jnp.zeros((near * TILE, LANES), jnp.bfloat16)


def partial_kernel(total_freq, total_steps, chips, *refs):
    count = (len(refs) - 3) // 2
    out_ref, pick_ref = refs[count : count + 2]
    history_ref, *index_refs = refs[count + 2 : -1]
    copies = [
        pltpu.make_async_copy(refs[i], refs[count + 2 + i], refs[-1].at[i]) for i in range(count)
    ]
    for copy in copies:
        copy.start()
    steps = history_ref.shape[0]
    rows = 2 * total_freq
    leaf = out_ref.shape[-1]
    leaves = history_ref.shape[1] // leaf
    row = iota((rows, steps), 0)
    step = lax.axis_index("freq") * steps + iota((rows, steps), 1)
    freq = ((row >> 1) + total_freq // 2) % total_freq * (total_steps // total_freq) + 1
    phase = (freq * step + (row & 1) * (total_steps // 4)) & (total_steps - 1)
    angle = 2.0 * math.pi / total_steps * phase.astype(jnp.float32)
    damping = jnp.exp(step.astype(jnp.float32) * (math.log(fall_total) / total_steps))
    weights = (damping * jnp.cos(angle) / math.sqrt(total_steps)).astype(jnp.bfloat16)
    for copy in copies:
        copy.wait()
    part = dot(weights, history_ref[...])
    for l in range(leaves):
        out_ref[pl.ds(l, rows, stride=leaves), :] = part[:, l * leaf : (l + 1) * leaf]
    plan(chips, pick_ref, *index_refs)


def block_kernel(tasks, pick_ref, gathered_ref, right_ref, left_ref, blocks_ref, out_ref, near_ref):
    columns = gathered_ref.shape[0]
    picked = dot(pick_ref[:, :columns], gathered_ref[...]).astype(jnp.bfloat16)
    half = out_ref.shape[0]
    extra = pick_ref[: 2 * half, columns:].astype(jnp.float32)
    pair = jnp.concatenate([picked[:half], picked[half : 2 * half]], 1)
    leaf = left_ref.shape[-1]
    own = iota((TILE, leaf), 0) % GROUP
    lane = iota((TILE, leaf), 1).astype(jnp.float32)
    coeffs = []
    for start in range(0, tasks, GROUP):
        rows = slice(2 * start, 2 * start + TILE)
        coeff = jnp.zeros((TILE, leaf), jnp.float32)
        for t in range(start, min(start + GROUP, tasks)):
            coeff = jnp.where(own == t - start, dot(pair[rows], right_ref[t]), coeff)
        coeffs.append(jnp.where(lane < extra[rows], coeff, 0.0).astype(jnp.bfloat16))
    for start, coeff in zip(range(0, tasks, GROUP), coeffs):
        rows = slice(2 * start, 2 * start + TILE)
        direct = jnp.zeros((TILE, leaf), jnp.float32)
        crossed = jnp.zeros((TILE, leaf), jnp.float32)
        for t in range(start, min(start + GROUP, tasks)):
            both = dot(coeff, left_ref[t], True)
            direct = jnp.where(own == t - start, both[:, :leaf], direct)
            crossed = jnp.where(own == t - start, both[:, leaf:], crossed)
        goal = extra[half + 2 * start : half + 2 * start + TILE]
        terms = turn(direct, crossed) + goal
        out_ref[rows, :] = terms.astype(jnp.bfloat16)
    leaves, near = blocks_ref.shape[:2]
    direct = jnp.zeros((TILE, leaf), jnp.float32)
    crossed = jnp.zeros((TILE, leaf), jnp.float32)
    for n in range(near):
        view = picked[2 * half + TILE * n : 2 * half + TILE * (n + 1)]
        for l in range(leaves):
            both = dot(view, blocks_ref[l, n], True)
            direct = direct + jnp.where(own == l, both[:, :leaf], 0.0)
            crossed = crossed + jnp.where(own == l, both[:, leaf:], 0.0)
    near_ref[...] = turn(direct, crossed)


def spectrum_kernel(shares_ref, out_ref):
    spectrum = jnp.sum(shares_ref[...], 0).astype(jnp.bfloat16)
    for chip in range(out_ref.shape[0]):
        out_ref[chip] = spectrum


def scatter_kernel(tasks, chips, terms_ref, out_ref):
    terms = terms_ref[...]
    columns = terms.shape[0]
    rows = columns // CORES
    spare = tasks // GROUP * TILE + tasks % GROUP
    lane = iota((1, terms.shape[1]), 1)
    wide = terms.astype(jnp.float32)

    def along(at):
        return jnp.where(lane < rows, wide[at : at + 1], wide[rows + at : rows + at + 1])

    goal = (along(spare) * GROUP + along(spare + 1)).astype(jnp.int32)
    code = (goal * 2 + lane // GROUP % 2)[:, :columns]
    row = iota((TILE, columns), 0)
    base = (lax.axis_index("core") * GROUP + row % GROUP) * 2 + row // GROUP
    place = jnp.concatenate(
        [
            jnp.where(code - chip * (CORES * TILE) == base, 1.0, 0.0)
            for chip in rotated(chips, first_chip(chips))
        ],
        0,
    )
    out_ref[...] = dot(place.astype(jnp.bfloat16), terms).astype(jnp.bfloat16)


def call(kernel, outs, spaces, scratch=(), limit=16, flops=0):
    return pl.pallas_call(
        kernel,
        out_shape=[jax.ShapeDtypeStruct(shape, dtype) for shape, dtype in outs],
        in_specs=[pl.BlockSpec(memory_space=space) for space in spaces],
        out_specs=[pl.BlockSpec(memory_space=pltpu.VMEM) for _ in outs],
        scratch_shapes=scratch,
        cost_estimate=pl.CostEstimate(flops=flops, transcendentals=0, bytes_accessed=2**20),
        compiler_params=pltpu.CompilerParams(vmem_limit_bytes=limit * 2**20),
    )


def per_device(
    history, near_blocks, near_leaves, far_left, far_right, far_ranks, far_targets, far_sources
):
    vmem = pltpu.VMEM
    freq_groups = lax.axis_size("freq")
    chips = lax.axis_size("chip")
    total_freq = far_ranks.shape[0] * freq_groups
    total_steps = history.shape[0] * freq_groups
    leaf = near_blocks.shape[-1]
    leaves = near_blocks.shape[1]
    near = near_blocks.shape[2]
    tasks = far_ranks.shape[1]
    slots = -(-tasks // GROUP) * GROUP

    arrays = (
        history,
        far_sources.reshape(1, tasks),
        far_ranks,
        far_targets.reshape(1, tasks),
        near_leaves.T,
    )
    partial, pick = call(
        functools.partial(partial_kernel, total_freq, total_steps, chips),
        [
            ((total_freq * TILE, leaf), jnp.float32),
            ((4 * slots + near * TILE, CORES * chips * TILE + LANES), jnp.bfloat16),
        ],
        [pl.ANY] * len(arrays),
        [
            *[pltpu.VMEM(array.shape, array.dtype) for array in arrays],
            pltpu.SemaphoreType.DMA((len(arrays),)),
        ],
        limit=60,
    )(*arrays)
    shares = lax.all_to_all(
        partial.reshape(total_freq, TILE, leaf),
        "freq",
        0,
        0,
        axis_index_groups=[rotated(freq_groups, freq_groups // 2)],
        tiled=True,
    )
    (copies,) = call(
        spectrum_kernel, [((chips, TILE, leaf), jnp.bfloat16)], [vmem], flops=20_000_000_000
    )(shares)
    same_core = lax.all_to_all(
        copies, "chip", 0, 0, axis_index_groups=[rotated(chips, first_chip(chips))], tiled=True
    )
    gathered = lax.all_gather(same_core, "core", axis=0, tiled=False)
    gathered = gathered.reshape(CORES * chips * TILE, leaf)

    terms, near_field = call(
        functools.partial(block_kernel, tasks),
        [((2 * slots, leaf), jnp.bfloat16), ((TILE, leaf), jnp.float32)],
        [vmem] * 5,
    )(
        pick,
        gathered,
        far_right[0].reshape(tasks, 2 * leaf, leaf),
        far_left[0].reshape(tasks, 2 * leaf, leaf),
        near_blocks[0].reshape(leaves, near, 2 * leaf, leaf),
    )

    both_terms = lax.all_gather(terms, "core", axis=0, tiled=True)
    (spread,) = call(
        functools.partial(scatter_kernel, tasks, chips),
        [((chips * TILE, leaf), jnp.bfloat16)],
        [vmem],
    )(both_terms)
    arrived = lax.all_to_all(
        spread.reshape(chips, TILE, leaf),
        "chip",
        0,
        0,
        axis_index_groups=[rotated(chips, first_chip(chips))],
        tiled=True,
    )

    field = near_field + jnp.sum(arrived.astype(jnp.float32), 0)
    return field.reshape(1, 2, leaves * leaf).astype(jnp.bfloat16)


def solution(mesh):
    freq_groups, elem_groups = mesh.devices.shape
    split = Mesh(
        mesh.devices.reshape(freq_groups, elem_groups // CORES, CORES), ("freq", "chip", "core")
    )
    elem = ("chip", "core")
    in_specs = (
        P("freq", elem),
        P("freq", elem, None, None, None, None),
        P(elem, None),
        P("freq", elem, None, None, None),
        P("freq", elem, None, None, None),
        P("freq", elem),
        P(elem),
        P(elem),
    )
    out_specs = P("freq", None, elem)
    return jax.shard_map(
        per_device, mesh=split, in_specs=in_specs, out_specs=out_specs, check_vma=False
    )
```

```python
import functools
import math

import jax
import jax.numpy as jnp
from jax import lax
from jax.experimental import pallas as pl
from jax.experimental.pallas import tpu as pltpu
from jax.sharding import Mesh
from jax.sharding import PartitionSpec as P

fall_total = 0.25
CORES = 2
GROUP = 8
TILE = 2 * GROUP
LANES = 128


def rotated(size, first):
    return [(i + first) % size for i in range(size)]


def first_chip(chips):
    return chips * 3 // 4 + 2


def dot(first_op, second_op, transposed=False):
    dims = (((1,), (1 if transposed else 0,)), ((), ()))
    return lax.dot_general(first_op, second_op, dims, preferred_element_type=jnp.float32)


def iota(shape, dim):
    return lax.broadcasted_iota(jnp.int32, shape, dim)


def times_i(tile):
    return jnp.concatenate([-tile[GROUP:], tile[:GROUP]], 0)


def leaf_codes(chunk, chips):
    at = chunk * LANES + iota((1, LANES), 1)
    core = at // (chips * TILE)
    chip = (at // TILE + first_chip(chips)) % chips
    return (chip * CORES + core) * TILE + at % GROUP * 2 + at // GROUP % 2


def plan(chips, pick_ref, sources_ref, ranks_ref, targets_ref, leaves_ref):
    tasks = sources_ref.shape[1]
    near, leaves = leaves_ref.shape
    rows = 2 * (-(-tasks // GROUP) * GROUP)
    row = iota((rows, LANES), 0)
    lane = iota((rows, LANES), 1)
    task = row // TILE * GROUP + row % GROUP
    part = row // GROUP % 2

    def by_row(ref):
        value = ref[...].astype(jnp.float32)
        found = jnp.where(iota((rows, tasks), 1) == task[:, :tasks], value, 0.0)
        return jnp.where(task < tasks, jnp.sum(found, 1, keepdims=True), -1.0)

    wanted = leaves_ref[...].astype(jnp.float32)
    own = iota((TILE, leaves), 1) == iota((TILE, leaves), 0) % GROUP
    listed = [
        jnp.sum(jnp.where(own, wanted[n : n + 1], 0.0), 1, keepdims=True) for n in range(near)
    ]
    near_part = iota((TILE, LANES), 0) // GROUP
    codes_of_rows = jnp.concatenate(
        [by_row(sources_ref).astype(jnp.int32) * 2 + part]
        + [leaf.astype(jnp.int32) * 2 + near_part for leaf in listed],
        0,
    )
    chunks = pick_ref.shape[1] // LANES - 2
    for chunk in range(chunks):
        pick_ref[:, chunk * LANES : (chunk + 1) * LANES] = jnp.where(
            codes_of_rows == leaf_codes(chunk, chips), 1.0, 0.0
        ).astype(jnp.bfloat16)
    target = jnp.sum(jnp.where(row == lane % rows, by_row(targets_ref), 0.0), 0, keepdims=True)
    target = target.astype(jnp.int32)
    spare = tasks // GROUP * TILE + tasks % GROUP
    goal = jnp.where(row == spare, target >> 3, jnp.where(row == spare + 1, target & 7, 0))
    extra = jnp.concatenate([by_row(ranks_ref), goal.astype(jnp.float32)], 1)
    pick_ref[:rows, chunks * LANES :] = extra.astype(jnp.bfloat16)
    pick_ref[rows:, chunks * LANES :] = jnp.zeros((near * TILE, 2 * LANES), jnp.bfloat16)


def partial_kernel(total_freq, total_steps, chips, *refs):
    count = (len(refs) - 3) // 2
    out_ref, pick_ref = refs[count : count + 2]
    history_ref, *index_refs = refs[count + 2 : -1]
    copies = [
        pltpu.make_async_copy(refs[i], refs[count + 2 + i], refs[-1].at[i]) for i in range(count)
    ]
    for copy in copies:
        copy.start()
    steps = history_ref.shape[0]
    rows = 2 * total_freq
    leaf = out_ref.shape[-1]
    leaves = history_ref.shape[1] // leaf
    row = iota((rows, steps), 0)
    step = lax.axis_index("freq") * steps + iota((rows, steps), 1)
    freq = ((row >> 1) + total_freq // 2) % total_freq * (total_steps // total_freq) + 1
    phase = (freq * step + (row & 1) * (total_steps // 4)) & (total_steps - 1)
    angle = 2.0 * math.pi / total_steps * phase.astype(jnp.float32)
    damping = jnp.exp(step.astype(jnp.float32) * (math.log(fall_total) / total_steps))
    weights = (damping * jnp.cos(angle) / math.sqrt(total_steps)).astype(jnp.bfloat16)
    for copy in copies:
        copy.wait()
    part = dot(weights, history_ref[...])
    for l in range(leaves):
        out_ref[pl.ds(l, rows, stride=leaves), :] = part[:, l * leaf : (l + 1) * leaf]
    plan(chips, pick_ref, *index_refs)


def block_kernel(tasks, pick_ref, gathered_ref, right_ref, left_ref, blocks_ref, out_ref, near_ref):
    columns = gathered_ref.shape[0]
    picked = dot(pick_ref[:, :columns], gathered_ref[...])
    extra = pick_ref[: out_ref.shape[0], columns:].astype(jnp.float32)
    leaf = left_ref.shape[-1]
    own = iota((TILE, leaf), 0) % GROUP
    lane = iota((TILE, leaf), 1).astype(jnp.float32)
    coeffs = []
    for start in range(0, tasks, GROUP):
        rows = slice(2 * start, 2 * start + TILE)
        coeff = jnp.zeros((TILE, leaf), jnp.float32)
        pair = jnp.concatenate([picked[rows], times_i(picked[rows])], 1).astype(jnp.bfloat16)
        for t in range(start, min(start + GROUP, tasks)):
            coeff = jnp.where(own == t - start, dot(pair, right_ref[t]), coeff)
        coeffs.append(jnp.where(lane < extra[rows, :leaf], coeff, 0.0).astype(jnp.bfloat16))
    for start, coeff in zip(range(0, tasks, GROUP), coeffs):
        rows = slice(2 * start, 2 * start + TILE)
        direct = jnp.zeros((TILE, leaf), jnp.float32)
        crossed = jnp.zeros((TILE, leaf), jnp.float32)
        for t in range(start, min(start + GROUP, tasks)):
            both = dot(coeff, left_ref[t], True)
            direct = jnp.where(own == t - start, both[:, :leaf], direct)
            crossed = jnp.where(own == t - start, both[:, leaf:], crossed)
        terms = direct + times_i(crossed) + extra[rows, leaf:]
        out_ref[rows, :] = terms.astype(jnp.bfloat16)
    leaves, near = blocks_ref.shape[:2]
    direct = jnp.zeros((TILE, leaf), jnp.float32)
    crossed = jnp.zeros((TILE, leaf), jnp.float32)
    for n in range(near):
        at = out_ref.shape[0] + TILE * n
        view = picked[at : at + TILE].astype(jnp.bfloat16)
        for l in range(leaves):
            both = dot(view, blocks_ref[l, n], True)
            direct = direct + jnp.where(own == l, both[:, :leaf], 0.0)
            crossed = crossed + jnp.where(own == l, both[:, leaf:], 0.0)
    near_ref[...] = direct + times_i(crossed)


def spectrum_kernel(shares_ref, out_ref):
    spectrum = jnp.sum(shares_ref[...], 0).astype(jnp.bfloat16)
    for chip in range(out_ref.shape[0]):
        out_ref[chip] = spectrum


def field_kernel(arrived_ref, near_ref, out_ref):
    total = near_ref[...] + jnp.sum(arrived_ref[...].astype(jnp.float32), 0)
    parts = [
        jnp.concatenate([total[l : l + 1], total[GROUP + l : GROUP + l + 1]], 0)
        for l in range(GROUP)
    ]
    out_ref[...] = jnp.concatenate(parts, 1).astype(jnp.bfloat16)


def scatter_kernel(tasks, chips, terms_ref, out_ref):
    terms = terms_ref[...]
    columns = terms.shape[0]
    rows = columns // CORES
    spare = tasks // GROUP * TILE + tasks % GROUP
    lane = iota((1, terms.shape[1]), 1)
    wide = terms.astype(jnp.float32)

    def along(at):
        return jnp.where(lane < rows, wide[at : at + 1], wide[rows + at : rows + at + 1])

    goal = (along(spare) * GROUP + along(spare + 1)).astype(jnp.int32)
    code = (goal * 2 + lane // GROUP % 2)[:, :columns]
    row = iota((TILE, columns), 0)
    base = (lax.axis_index("core") * GROUP + row % GROUP) * 2 + row // GROUP
    place = jnp.concatenate(
        [
            jnp.where(code - chip * (CORES * TILE) == base, 1.0, 0.0)
            for chip in rotated(chips, first_chip(chips))
        ],
        0,
    )
    out_ref[...] = dot(place.astype(jnp.bfloat16), terms).astype(jnp.bfloat16)


def call(kernel, outs, spaces, scratch=(), limit=16, flops=0):
    return pl.pallas_call(
        kernel,
        out_shape=[jax.ShapeDtypeStruct(shape, dtype) for shape, dtype in outs],
        in_specs=[pl.BlockSpec(memory_space=space) for space in spaces],
        out_specs=[pl.BlockSpec(memory_space=pltpu.VMEM) for _ in outs],
        scratch_shapes=scratch,
        cost_estimate=pl.CostEstimate(flops=flops, transcendentals=0, bytes_accessed=2**20),
        compiler_params=pltpu.CompilerParams(vmem_limit_bytes=limit * 2**20),
    )


def per_device(
    history, near_blocks, near_leaves, far_left, far_right, far_ranks, far_targets, far_sources
):
    vmem = pltpu.VMEM
    freq_groups = lax.axis_size("freq")
    chips = lax.axis_size("chip")
    total_freq = far_ranks.shape[0] * freq_groups
    total_steps = history.shape[0] * freq_groups
    leaf = near_blocks.shape[-1]
    leaves = near_blocks.shape[1]
    near = near_blocks.shape[2]
    tasks = far_ranks.shape[1]
    slots = -(-tasks // GROUP) * GROUP

    arrays = (
        history,
        far_sources.reshape(1, tasks),
        far_ranks,
        far_targets.reshape(1, tasks),
        near_leaves.T,
    )
    partial, pick = call(
        functools.partial(partial_kernel, total_freq, total_steps, chips),
        [
            ((total_freq * TILE, leaf), jnp.float32),
            ((2 * slots + near * TILE, CORES * chips * TILE + 2 * LANES), jnp.bfloat16),
        ],
        [pl.ANY] * len(arrays),
        [
            *[pltpu.VMEM(array.shape, array.dtype) for array in arrays],
            pltpu.SemaphoreType.DMA((len(arrays),)),
        ],
    )(*[pltpu.with_memory_space_constraint(array, pltpu.HBM) for array in arrays])
    shares = lax.all_to_all(
        partial.reshape(total_freq, TILE, leaf),
        "freq",
        0,
        0,
        axis_index_groups=[rotated(freq_groups, freq_groups // 2)],
        tiled=True,
    )
    (copies,) = call(
        spectrum_kernel, [((chips, TILE, leaf), jnp.bfloat16)], [vmem], flops=20_000_000_000
    )(shares)
    same_core = lax.all_to_all(
        copies, "chip", 0, 0, axis_index_groups=[rotated(chips, first_chip(chips))], tiled=True
    )
    gathered = lax.all_gather(same_core, "core", axis=0, tiled=False)
    gathered = gathered.reshape(CORES * chips * TILE, leaf)

    terms, near_field = call(
        functools.partial(block_kernel, tasks),
        [((2 * slots, leaf), jnp.bfloat16), ((TILE, leaf), jnp.float32)],
        [vmem] * 5,
    )(
        pick,
        gathered,
        far_right[0].reshape(tasks, 2 * leaf, leaf),
        far_left[0].reshape(tasks, 2 * leaf, leaf),
        near_blocks[0].reshape(leaves, near, 2 * leaf, leaf),
    )

    both_terms = lax.all_gather(terms, "core", axis=0, tiled=True)
    (spread,) = call(
        functools.partial(scatter_kernel, tasks, chips),
        [((chips * TILE, leaf), jnp.bfloat16)],
        [vmem],
    )(both_terms)
    arrived = lax.all_to_all(
        spread.reshape(chips, TILE, leaf),
        "chip",
        0,
        0,
        axis_index_groups=[rotated(chips, first_chip(chips))],
        tiled=True,
    )

    (field,) = call(field_kernel, [((2, leaves * leaf), jnp.bfloat16)], [vmem, vmem])(
        arrived, near_field
    )
    return field[None]


def solution(mesh):
    freq_groups, elem_groups = mesh.devices.shape
    split = Mesh(
        mesh.devices.reshape(freq_groups, elem_groups // CORES, CORES), ("freq", "chip", "core")
    )
    elem = ("chip", "core")
    in_specs = (
        P("freq", elem),
        P("freq", elem, None, None, None, None),
        P(elem, None),
        P("freq", elem, None, None, None),
        P("freq", elem, None, None, None),
        P("freq", elem),
        P(elem),
        P(elem),
    )
    out_specs = P("freq", None, elem)
    return jax.shard_map(
        per_device, mesh=split, in_specs=in_specs, out_specs=out_specs, check_vma=False
    )
```

```python
import functools
import math

import jax
import jax.numpy as jnp
from jax import lax
from jax.experimental import pallas as pl
from jax.experimental.pallas import tpu as pltpu
from jax.sharding import Mesh
from jax.sharding import PartitionSpec as P

fall_total = 0.25
CORES = 2
GROUP = 8
TILE = 2 * GROUP
LANES = 128


def rotated(size, first):
    return [(i + first) % size for i in range(size)]


def first_chip(chips):
    return chips // 2 + 2


def dot(first_op, second_op, transposed=False):
    dims = (((1,), (1 if transposed else 0,)), ((), ()))
    return lax.dot_general(first_op, second_op, dims, preferred_element_type=jnp.float32)


def iota(shape, dim):
    return lax.broadcasted_iota(jnp.int32, shape, dim)


def times_i(tile):
    return jnp.concatenate([-tile[GROUP:], tile[:GROUP]], 0)


def leaf_codes(chunk, chips):
    at = chunk * LANES + iota((1, LANES), 1)
    core = at // (chips * TILE)
    chip = (at // TILE + first_chip(chips)) % chips
    return (chip * CORES + core) * TILE + at % GROUP * 2 + at // GROUP % 2


def plan(chips, pick_ref, sources_ref, ranks_ref, targets_ref, leaves_ref):
    tasks = sources_ref.shape[1]
    near, leaves = leaves_ref.shape
    rows = 2 * (-(-tasks // GROUP) * GROUP)
    row = iota((rows, LANES), 0)
    lane = iota((rows, LANES), 1)
    task = row // TILE * GROUP + row % GROUP
    part = row // GROUP % 2

    def by_row(ref):
        value = ref[...].astype(jnp.float32)
        found = jnp.where(iota((rows, tasks), 1) == task[:, :tasks], value, 0.0)
        return jnp.where(task < tasks, jnp.sum(found, 1, keepdims=True), -1.0)

    wanted = leaves_ref[...].astype(jnp.float32)
    own = iota((TILE, leaves), 1) == iota((TILE, leaves), 0) % GROUP
    listed = [
        jnp.sum(jnp.where(own, wanted[n : n + 1], 0.0), 1, keepdims=True) for n in range(near)
    ]
    near_part = iota((TILE, LANES), 0) // GROUP
    codes_of_rows = jnp.concatenate(
        [by_row(sources_ref).astype(jnp.int32) * 2 + part]
        + [leaf.astype(jnp.int32) * 2 + near_part for leaf in listed],
        0,
    )
    chunks = pick_ref.shape[1] // LANES - 2
    for chunk in range(chunks):
        pick_ref[:, chunk * LANES : (chunk + 1) * LANES] = jnp.where(
            codes_of_rows == leaf_codes(chunk, chips), 1.0, 0.0
        ).astype(jnp.bfloat16)
    target = jnp.sum(jnp.where(row == lane % rows, by_row(targets_ref), 0.0), 0, keepdims=True)
    target = target.astype(jnp.int32)
    spare = tasks // GROUP * TILE + tasks % GROUP
    goal = jnp.where(row == spare, target >> 3, jnp.where(row == spare + 1, target & 7, 0))
    extra = jnp.concatenate([by_row(ranks_ref), goal.astype(jnp.float32)], 1)
    pick_ref[:rows, chunks * LANES :] = extra.astype(jnp.bfloat16)
    pick_ref[rows:, chunks * LANES :] = jnp.zeros((near * TILE, 2 * LANES), jnp.bfloat16)


def partial_kernel(total_freq, total_steps, chips, *refs):
    count = (len(refs) - 3) // 2
    out_ref, pick_ref = refs[count : count + 2]
    history_ref, *index_refs = refs[count + 2 : -1]
    copies = [
        pltpu.make_async_copy(refs[i], refs[count + 2 + i], refs[-1].at[i]) for i in range(count)
    ]
    for copy in copies:
        copy.start()
    steps = history_ref.shape[0]
    rows = 2 * total_freq
    leaf = out_ref.shape[-1]
    leaves = history_ref.shape[1] // leaf
    row = iota((rows, steps), 0)
    step = lax.axis_index("freq") * steps + iota((rows, steps), 1)
    freq = ((row >> 1) + total_freq // 2) % total_freq * (total_steps // total_freq) + 1
    phase = (freq * step + (row & 1) * (total_steps // 4)) & (total_steps - 1)
    angle = 2.0 * math.pi / total_steps * phase.astype(jnp.float32)
    damping = jnp.exp(step.astype(jnp.float32) * (math.log(fall_total) / total_steps))
    weights = (damping * jnp.cos(angle) / math.sqrt(total_steps)).astype(jnp.bfloat16)
    copies[0].wait()
    part = dot(weights, history_ref[...])
    for l in range(leaves):
        out_ref[pl.ds(l, rows, stride=leaves), :] = part[:, l * leaf : (l + 1) * leaf]
    for copy in copies[1:]:
        copy.wait()
    plan(chips, pick_ref, *index_refs)


def block_kernel(tasks, pick_ref, gathered_ref, right_ref, left_ref, blocks_ref, out_ref, near_ref):
    columns = gathered_ref.shape[0]
    picked = dot(pick_ref[:, :columns], gathered_ref[...])
    extra = pick_ref[: out_ref.shape[0], columns:].astype(jnp.float32)
    leaf = left_ref.shape[-1]
    own = iota((TILE, leaf), 0) % GROUP
    lane = iota((TILE, leaf), 1).astype(jnp.float32)
    leaves, near = blocks_ref.shape[:2]
    views = [
        picked[out_ref.shape[0] + TILE * n : out_ref.shape[0] + TILE * (n + 1)].astype(jnp.bfloat16)
        for n in range(near)
    ]

    def near_part(n):
        kept = jnp.zeros((TILE, 2 * leaf), jnp.float32)
        wide_own = iota((TILE, 2 * leaf), 0) % GROUP
        for l in range(leaves):
            kept = jnp.where(wide_own == l, dot(views[n], blocks_ref[l, n], True), kept)
        return kept

    groups = [
        (slice(2 * start, 2 * start + TILE), start, min(start + GROUP, tasks))
        for start in range(0, tasks, GROUP)
    ]
    coeffs, near_sums = [], near_part(0)
    for rows, start, stop in groups:
        coeff = jnp.zeros((TILE, leaf), jnp.float32)
        pair = jnp.concatenate([picked[rows], times_i(picked[rows])], 1).astype(jnp.bfloat16)
        for t in range(start, stop):
            coeff = jnp.where(own == t - start, dot(pair, right_ref[t]), coeff)
        coeffs.append(jnp.where(lane < extra[rows, :leaf], coeff, 0.0).astype(jnp.bfloat16))
    for n in range(1, near):
        near_sums = near_sums + near_part(n)
    for (rows, start, stop), coeff in zip(groups, coeffs):
        direct = jnp.zeros((TILE, leaf), jnp.float32)
        crossed = jnp.zeros((TILE, leaf), jnp.float32)
        for t in range(start, stop):
            both = dot(coeff, left_ref[t], True)
            direct = jnp.where(own == t - start, both[:, :leaf], direct)
            crossed = jnp.where(own == t - start, both[:, leaf:], crossed)
        terms = direct + times_i(crossed) + extra[rows, leaf:]
        out_ref[rows, :] = terms.astype(jnp.bfloat16)
    near_ref[...] = near_sums[:, :leaf] + times_i(near_sums[:, leaf:])


def spectrum_kernel(shares_ref, out_ref):
    spectrum = jnp.sum(shares_ref[...], 0).astype(jnp.bfloat16)
    for chip in range(out_ref.shape[0]):
        out_ref[chip] = spectrum


def field_kernel(arrived_ref, near_ref, out_ref):
    total = near_ref[...] + jnp.sum(arrived_ref[...].astype(jnp.float32), 0)
    parts = [
        jnp.concatenate([total[l : l + 1], total[GROUP + l : GROUP + l + 1]], 0)
        for l in range(GROUP)
    ]
    out_ref[...] = jnp.concatenate(parts, 1).astype(jnp.bfloat16)


def scatter_kernel(tasks, chips, terms_ref, out_ref):
    terms = terms_ref[...]
    columns = terms.shape[0]
    rows = columns // CORES
    spare = tasks // GROUP * TILE + tasks % GROUP
    lane = iota((1, terms.shape[1]), 1)
    wide = terms.astype(jnp.float32)

    def along(at):
        return jnp.where(lane < rows, wide[at : at + 1], wide[rows + at : rows + at + 1])

    goal = (along(spare) * GROUP + along(spare + 1)).astype(jnp.int32)
    code = (goal * 2 + lane // GROUP % 2)[:, :columns]
    row = iota((TILE, columns), 0)
    base = (lax.axis_index("core") * GROUP + row % GROUP) * 2 + row // GROUP
    place = jnp.concatenate(
        [
            jnp.where(code - chip * (CORES * TILE) == base, 1.0, 0.0)
            for chip in rotated(chips, first_chip(chips))
        ],
        0,
    )
    out_ref[...] = dot(place.astype(jnp.bfloat16), terms).astype(jnp.bfloat16)


def call(kernel, outs, spaces, scratch=(), limit=16, flops=0):
    return pl.pallas_call(
        kernel,
        out_shape=[jax.ShapeDtypeStruct(shape, dtype) for shape, dtype in outs],
        in_specs=[pl.BlockSpec(memory_space=space) for space in spaces],
        out_specs=[pl.BlockSpec(memory_space=pltpu.VMEM) for _ in outs],
        scratch_shapes=scratch,
        cost_estimate=pl.CostEstimate(flops=flops, transcendentals=0, bytes_accessed=2**20),
        compiler_params=pltpu.CompilerParams(vmem_limit_bytes=limit * 2**20),
    )


def per_device(
    history, near_blocks, near_leaves, far_left, far_right, far_ranks, far_targets, far_sources
):
    vmem = pltpu.VMEM
    freq_groups = lax.axis_size("freq")
    chips = lax.axis_size("chip")
    total_freq = far_ranks.shape[0] * freq_groups
    total_steps = history.shape[0] * freq_groups
    leaf = near_blocks.shape[-1]
    leaves = near_blocks.shape[1]
    near = near_blocks.shape[2]
    tasks = far_ranks.shape[1]
    slots = -(-tasks // GROUP) * GROUP

    arrays = (
        history,
        far_sources.reshape(1, tasks),
        far_ranks,
        far_targets.reshape(1, tasks),
        near_leaves.T,
    )
    partial, pick = call(
        functools.partial(partial_kernel, total_freq, total_steps, chips),
        [
            ((total_freq * TILE, leaf), jnp.float32),
            ((2 * slots + near * TILE, CORES * chips * TILE + 2 * LANES), jnp.bfloat16),
        ],
        [pl.ANY] * len(arrays),
        [
            *[pltpu.VMEM(array.shape, array.dtype) for array in arrays],
            pltpu.SemaphoreType.DMA((len(arrays),)),
        ],
    )(*[pltpu.with_memory_space_constraint(array, pltpu.HBM) for array in arrays])
    shares = lax.all_to_all(
        partial.reshape(total_freq, TILE, leaf),
        "freq",
        0,
        0,
        axis_index_groups=[rotated(freq_groups, freq_groups // 2)],
        tiled=True,
    )
    (copies,) = call(
        spectrum_kernel, [((chips, TILE, leaf), jnp.bfloat16)], [vmem], flops=20_000_000_000
    )(shares)
    same_core = lax.all_to_all(
        copies, "chip", 0, 0, axis_index_groups=[rotated(chips, first_chip(chips))], tiled=True
    )
    gathered = lax.all_gather(same_core, "core", axis=0, tiled=False)
    gathered = gathered.reshape(CORES * chips * TILE, leaf)

    terms, near_field = call(
        functools.partial(block_kernel, tasks),
        [((2 * slots, leaf), jnp.bfloat16), ((TILE, leaf), jnp.float32)],
        [vmem] * 5,
    )(
        pick,
        gathered,
        far_right[0].reshape(tasks, 2 * leaf, leaf),
        far_left[0].reshape(tasks, 2 * leaf, leaf),
        near_blocks[0].reshape(leaves, near, 2 * leaf, leaf),
    )

    both_terms = lax.all_gather(terms, "core", axis=0, tiled=True)
    (spread,) = call(
        functools.partial(scatter_kernel, tasks, chips),
        [((chips * TILE, leaf), jnp.bfloat16)],
        [vmem],
    )(both_terms)
    arrived = lax.all_to_all(
        spread.reshape(chips, TILE, leaf),
        "chip",
        0,
        0,
        axis_index_groups=[rotated(chips, first_chip(chips))],
        tiled=True,
    )

    (field,) = call(field_kernel, [((2, leaves * leaf), jnp.bfloat16)], [vmem, vmem])(
        arrived, near_field
    )
    return field[None]


def solution(mesh):
    freq_groups, elem_groups = mesh.devices.shape
    split = Mesh(
        mesh.devices.reshape(freq_groups, elem_groups // CORES, CORES), ("freq", "chip", "core")
    )
    elem = ("chip", "core")
    in_specs = (
        P("freq", elem),
        P("freq", elem, None, None, None, None),
        P(elem, None),
        P("freq", elem, None, None, None),
        P("freq", elem, None, None, None),
        P("freq", elem),
        P(elem),
        P(elem),
    )
    out_specs = P("freq", None, elem)
    return jax.shard_map(
        per_device, mesh=split, in_specs=in_specs, out_specs=out_specs, check_vma=False
    )
```

```python
import functools
import math

import jax
import jax.numpy as jnp
from jax import lax
from jax.experimental import pallas as pl
from jax.experimental.pallas import tpu as pltpu
from jax.sharding import Mesh
from jax.sharding import PartitionSpec as P

fall_total = 0.25
CORES = 2
GROUP = 8
TILE = 2 * GROUP
LANES = 128


def rotated(size, first):
    return [(i + first) % size for i in range(size)]


def first_chip(chips):
    return chips - 1


def dot(first_op, second_op, transposed=False):
    dims = (((1,), (1 if transposed else 0,)), ((), ()))
    return lax.dot_general(first_op, second_op, dims, preferred_element_type=jnp.float32)


def iota(shape, dim):
    return lax.broadcasted_iota(jnp.int32, shape, dim)


def times_i(tile):
    return jnp.concatenate([-tile[GROUP:], tile[:GROUP]], 0)


def leaf_codes(chunk, chips):
    at = chunk * LANES + iota((1, LANES), 1)
    core = at // (chips * TILE)
    chip = (at // TILE + first_chip(chips)) % chips
    return (chip * CORES + core) * TILE + at % GROUP * 2 + at // GROUP % 2


def plan(chips, pick_ref, sources_ref, ranks_ref, targets_ref, leaves_ref):
    tasks = sources_ref.shape[1]
    near, leaves = leaves_ref.shape
    rows = 2 * (-(-tasks // GROUP) * GROUP)
    row = iota((rows, LANES), 0)
    lane = iota((rows, LANES), 1)
    task = row // TILE * GROUP + row % GROUP
    part = row // GROUP % 2

    def by_row(ref):
        value = ref[...].astype(jnp.float32)
        found = jnp.where(iota((rows, tasks), 1) == task[:, :tasks], value, 0.0)
        return jnp.where(task < tasks, jnp.sum(found, 1, keepdims=True), -1.0)

    wanted = leaves_ref[...].astype(jnp.float32)
    own = iota((TILE, leaves), 1) == iota((TILE, leaves), 0) % GROUP
    listed = [
        jnp.sum(jnp.where(own, wanted[n : n + 1], 0.0), 1, keepdims=True) for n in range(near)
    ]
    near_part = iota((TILE, LANES), 0) // GROUP
    codes_of_rows = jnp.concatenate(
        [by_row(sources_ref).astype(jnp.int32) * 2 + part]
        + [leaf.astype(jnp.int32) * 2 + near_part for leaf in listed],
        0,
    )
    chunks = pick_ref.shape[1] // LANES - 2
    for chunk in range(chunks):
        pick_ref[:, chunk * LANES : (chunk + 1) * LANES] = jnp.where(
            codes_of_rows == leaf_codes(chunk, chips), 1.0, 0.0
        ).astype(jnp.bfloat16)
    target = jnp.sum(jnp.where(row == lane % rows, by_row(targets_ref), 0.0), 0, keepdims=True)
    target = target.astype(jnp.int32)
    spare = tasks // GROUP * TILE + tasks % GROUP
    goal = jnp.where(row == spare, target >> 3, jnp.where(row == spare + 1, target & 7, 0))
    extra = jnp.concatenate([by_row(ranks_ref), goal.astype(jnp.float32)], 1)
    pick_ref[:rows, chunks * LANES :] = extra.astype(jnp.bfloat16)
    pick_ref[rows:, chunks * LANES :] = jnp.zeros((near * TILE, 2 * LANES), jnp.bfloat16)


def partial_kernel(total_freq, total_steps, chips, *refs):
    count = (len(refs) - 3) // 2
    out_ref, pick_ref = refs[count : count + 2]
    history_ref, *index_refs = refs[count + 2 : -1]
    copies = [
        pltpu.make_async_copy(refs[i], refs[count + 2 + i], refs[-1].at[i]) for i in range(count)
    ]
    for copy in copies:
        copy.start()
    steps = history_ref.shape[0]
    rows = 2 * total_freq
    leaf = out_ref.shape[-1]
    leaves = history_ref.shape[1] // leaf
    row = iota((rows, steps), 0)
    step = lax.axis_index("freq") * steps + iota((rows, steps), 1)
    freq = ((row >> 1) + total_freq // 2) % total_freq * (total_steps // total_freq) + 1
    phase = (freq * step + (row & 1) * (total_steps // 4)) & (total_steps - 1)
    angle = 2.0 * math.pi / total_steps * phase.astype(jnp.float32)
    damping = jnp.exp(step.astype(jnp.float32) * (math.log(fall_total) / total_steps))
    weights = (damping * jnp.cos(angle) / math.sqrt(total_steps)).astype(jnp.bfloat16)
    for copy in copies:
        copy.wait()
    part = dot(weights, history_ref[...])
    for l in range(leaves):
        out_ref[pl.ds(l, rows, stride=leaves), :] = part[:, l * leaf : (l + 1) * leaf]
    plan(chips, pick_ref, *index_refs)


def block_kernel(tasks, pick_ref, gathered_ref, right_ref, left_ref, blocks_ref, out_ref, near_ref):
    columns = gathered_ref.shape[0]
    picked = dot(pick_ref[:, :columns], gathered_ref[...])
    extra = pick_ref[: out_ref.shape[0], columns:].astype(jnp.float32)
    leaf = left_ref.shape[-1]
    own = iota((TILE, leaf), 0) % GROUP
    lane = iota((TILE, leaf), 1).astype(jnp.float32)
    leaves, near = blocks_ref.shape[:2]
    views = [
        picked[out_ref.shape[0] + TILE * n : out_ref.shape[0] + TILE * (n + 1)].astype(jnp.bfloat16)
        for n in range(near)
    ]

    def near_part(n):
        kept = jnp.zeros((TILE, 2 * leaf), jnp.float32)
        wide_own = iota((TILE, 2 * leaf), 0) % GROUP
        for l in range(leaves):
            kept = jnp.where(wide_own == l, dot(views[n], blocks_ref[l, n], True), kept)
        return kept

    groups = [
        (slice(2 * start, 2 * start + TILE), start, min(start + GROUP, tasks))
        for start in range(0, tasks, GROUP)
    ]
    coeffs, near_sums = [], near_part(0)
    for rows, start, stop in groups:
        coeff = jnp.zeros((TILE, leaf), jnp.float32)
        pair = jnp.concatenate([picked[rows], times_i(picked[rows])], 1).astype(jnp.bfloat16)
        for t in range(start, stop):
            coeff = jnp.where(own == t - start, dot(pair, right_ref[t]), coeff)
        coeffs.append(jnp.where(lane < extra[rows, :leaf], coeff, 0.0).astype(jnp.bfloat16))
    for n in range(1, near):
        near_sums = near_sums + near_part(n)
    for (rows, start, stop), coeff in zip(groups, coeffs):
        direct = jnp.zeros((TILE, leaf), jnp.float32)
        crossed = jnp.zeros((TILE, leaf), jnp.float32)
        for t in range(start, stop):
            both = dot(coeff, left_ref[t], True)
            direct = jnp.where(own == t - start, both[:, :leaf], direct)
            crossed = jnp.where(own == t - start, both[:, leaf:], crossed)
        terms = direct + times_i(crossed) + extra[rows, leaf:]
        out_ref[rows, :] = terms.astype(jnp.bfloat16)
    near_ref[...] = near_sums[:, :leaf] + times_i(near_sums[:, leaf:])


def spectrum_kernel(shares_ref, out_ref):
    spectrum = jnp.sum(shares_ref[...], 0).astype(jnp.bfloat16)
    for chip in range(out_ref.shape[0]):
        out_ref[chip] = spectrum


def field_kernel(arrived_ref, near_ref, out_ref):
    total = near_ref[...] + jnp.sum(arrived_ref[...].astype(jnp.float32), 0)
    parts = [
        jnp.concatenate([total[l : l + 1], total[GROUP + l : GROUP + l + 1]], 0)
        for l in range(GROUP)
    ]
    out_ref[...] = jnp.concatenate(parts, 1).astype(jnp.bfloat16)


def scatter_kernel(tasks, chips, terms_ref, out_ref):
    terms = terms_ref[...]
    columns = terms.shape[0]
    rows = columns // CORES
    spare = tasks // GROUP * TILE + tasks % GROUP
    lane = iota((1, terms.shape[1]), 1)
    wide = terms.astype(jnp.float32)

    def along(at):
        return jnp.where(lane < rows, wide[at : at + 1], wide[rows + at : rows + at + 1])

    goal = (along(spare) * GROUP + along(spare + 1)).astype(jnp.int32)
    code = (goal * 2 + lane // GROUP % 2)[:, :columns]
    row = iota((TILE, columns), 0)
    base = (lax.axis_index("core") * GROUP + row % GROUP) * 2 + row // GROUP
    place = jnp.concatenate(
        [
            jnp.where(code - chip * (CORES * TILE) == base, 1.0, 0.0)
            for chip in rotated(chips, first_chip(chips))
        ],
        0,
    )
    out_ref[...] = dot(place.astype(jnp.bfloat16), terms).astype(jnp.bfloat16)


def call(kernel, outs, spaces, scratch=(), limit=16, flops=0):
    return pl.pallas_call(
        kernel,
        out_shape=[jax.ShapeDtypeStruct(shape, dtype) for shape, dtype in outs],
        in_specs=[pl.BlockSpec(memory_space=space) for space in spaces],
        out_specs=[pl.BlockSpec(memory_space=pltpu.VMEM) for _ in outs],
        scratch_shapes=scratch,
        cost_estimate=pl.CostEstimate(flops=flops, transcendentals=0, bytes_accessed=2**20),
        compiler_params=pltpu.CompilerParams(vmem_limit_bytes=limit * 2**20),
    )


def per_device(
    history, near_blocks, near_leaves, far_left, far_right, far_ranks, far_targets, far_sources
):
    vmem = pltpu.VMEM
    freq_groups = lax.axis_size("freq")
    chips = lax.axis_size("chip")
    total_freq = far_ranks.shape[0] * freq_groups
    total_steps = history.shape[0] * freq_groups
    leaf = near_blocks.shape[-1]
    leaves = near_blocks.shape[1]
    near = near_blocks.shape[2]
    tasks = far_ranks.shape[1]
    slots = -(-tasks // GROUP) * GROUP

    arrays = (
        history,
        far_sources.reshape(1, tasks),
        far_ranks,
        far_targets.reshape(1, tasks),
        near_leaves.T,
    )
    partial, pick = call(
        functools.partial(partial_kernel, total_freq, total_steps, chips),
        [
            ((total_freq * TILE, leaf), jnp.float32),
            ((2 * slots + near * TILE, CORES * chips * TILE + 2 * LANES), jnp.bfloat16),
        ],
        [pl.ANY] * len(arrays),
        [
            *[pltpu.VMEM(array.shape, array.dtype) for array in arrays],
            pltpu.SemaphoreType.DMA((len(arrays),)),
        ],
    )(*[pltpu.with_memory_space_constraint(array, pltpu.HBM) for array in arrays])
    shares = lax.all_to_all(
        partial.reshape(total_freq, TILE, leaf),
        "freq",
        0,
        0,
        axis_index_groups=[rotated(freq_groups, freq_groups // 2)],
        tiled=True,
    )
    (copies,) = call(
        spectrum_kernel, [((chips, TILE, leaf), jnp.bfloat16)], [vmem], flops=20_000_000_000
    )(shares)
    same_core = lax.all_to_all(
        copies, "chip", 0, 0, axis_index_groups=[rotated(chips, first_chip(chips))], tiled=True
    )
    gathered = lax.all_gather(same_core, "core", axis=0, tiled=False)
    gathered = gathered.reshape(CORES * chips * TILE, leaf)

    terms, near_field = call(
        functools.partial(block_kernel, tasks),
        [((2 * slots, leaf), jnp.bfloat16), ((TILE, leaf), jnp.float32)],
        [vmem] * 5,
    )(
        pick,
        gathered,
        far_right[0].reshape(tasks, 2 * leaf, leaf),
        far_left[0].reshape(tasks, 2 * leaf, leaf),
        near_blocks[0].reshape(leaves, near, 2 * leaf, leaf),
    )

    both_terms = lax.all_gather(terms, "core", axis=0, tiled=True)
    (spread,) = call(
        functools.partial(scatter_kernel, tasks, chips),
        [((chips * TILE, leaf), jnp.bfloat16)],
        [vmem],
    )(both_terms)
    arrived = lax.all_to_all(
        spread.reshape(chips, TILE, leaf),
        "chip",
        0,
        0,
        axis_index_groups=[rotated(chips, first_chip(chips))],
        tiled=True,
    )

    (field,) = call(field_kernel, [((2, leaves * leaf), jnp.bfloat16)], [vmem, vmem])(
        arrived, near_field
    )
    return field[None]


def solution(mesh):
    freq_groups, elem_groups = mesh.devices.shape
    split = Mesh(
        mesh.devices.reshape(freq_groups, elem_groups // CORES, CORES), ("freq", "chip", "core")
    )
    elem = ("chip", "core")
    in_specs = (
        P("freq", elem),
        P("freq", elem, None, None, None, None),
        P(elem, None),
        P("freq", elem, None, None, None),
        P("freq", elem, None, None, None),
        P("freq", elem),
        P(elem),
        P(elem),
    )
    out_specs = P("freq", None, elem)
    return jax.shard_map(
        per_device, mesh=split, in_specs=in_specs, out_specs=out_specs, check_vma=False
    )
```

```python
import functools
import math

import jax
import jax.numpy as jnp
from jax import lax
from jax.experimental import pallas as pl
from jax.experimental.pallas import tpu as pltpu
from jax.sharding import Mesh
from jax.sharding import PartitionSpec as P

fall_total = 0.25
CORES = 2
GROUP = 8
TILE = 2 * GROUP
LANES = 128


def rotated(size, first):
    return [(i + first) % size for i in range(size)]


def first_chip(chips):
    return chips - 2


def dot(first_op, second_op, transposed=False):
    dims = (((1,), (1 if transposed else 0,)), ((), ()))
    return lax.dot_general(first_op, second_op, dims, preferred_element_type=jnp.float32)


def iota(shape, dim):
    return lax.broadcasted_iota(jnp.int32, shape, dim)


def times_i(tile):
    return jnp.concatenate([-tile[GROUP:], tile[:GROUP]], 0)


def leaf_codes(chunk, chips):
    at = chunk * LANES + iota((1, LANES), 1)
    core = at // (chips * TILE)
    chip = (at // TILE + first_chip(chips)) % chips
    return (chip * CORES + core) * TILE + at % GROUP * 2 + at // GROUP % 2


def plan(chips, pick_ref, sources_ref, ranks_ref, targets_ref, leaves_ref):
    tasks = sources_ref.shape[1]
    near, leaves = leaves_ref.shape
    rows = 2 * (-(-tasks // GROUP) * GROUP)
    row = iota((rows, LANES), 0)
    lane = iota((rows, LANES), 1)
    task = row // TILE * GROUP + row % GROUP
    part = row // GROUP % 2

    def by_row(ref):
        value = ref[...].astype(jnp.float32)
        found = jnp.where(iota((rows, tasks), 1) == task[:, :tasks], value, 0.0)
        return jnp.where(task < tasks, jnp.sum(found, 1, keepdims=True), -1.0)

    wanted = leaves_ref[...].astype(jnp.float32)
    own = iota((TILE, leaves), 1) == iota((TILE, leaves), 0) % GROUP
    listed = [
        jnp.sum(jnp.where(own, wanted[n : n + 1], 0.0), 1, keepdims=True) for n in range(near)
    ]
    near_part = iota((TILE, LANES), 0) // GROUP
    codes_of_rows = jnp.concatenate(
        [by_row(sources_ref).astype(jnp.int32) * 2 + part]
        + [leaf.astype(jnp.int32) * 2 + near_part for leaf in listed],
        0,
    )
    chunks = pick_ref.shape[1] // LANES - 2
    for chunk in range(chunks):
        pick_ref[:, chunk * LANES : (chunk + 1) * LANES] = jnp.where(
            codes_of_rows == leaf_codes(chunk, chips), 1.0, 0.0
        ).astype(jnp.bfloat16)
    target = jnp.sum(jnp.where(row == lane % rows, by_row(targets_ref), 0.0), 0, keepdims=True)
    target = target.astype(jnp.int32)
    spare = tasks // GROUP * TILE + tasks % GROUP
    goal = jnp.where(row == spare, target >> 3, jnp.where(row == spare + 1, target & 7, 0))
    extra = jnp.concatenate([by_row(ranks_ref), goal.astype(jnp.float32)], 1)
    pick_ref[:rows, chunks * LANES :] = extra.astype(jnp.bfloat16)
    pick_ref[rows:, chunks * LANES :] = jnp.zeros((near * TILE, 2 * LANES), jnp.bfloat16)


def partial_kernel(total_freq, total_steps, chips, *refs):
    count = (len(refs) - 3) // 2
    out_ref, pick_ref = refs[count : count + 2]
    history_ref, *index_refs = refs[count + 2 : -1]
    copies = [
        pltpu.make_async_copy(refs[i], refs[count + 2 + i], refs[-1].at[i]) for i in range(count)
    ]
    for copy in copies:
        copy.start()
    steps = history_ref.shape[0]
    rows = 2 * total_freq
    leaf = out_ref.shape[-1]
    leaves = history_ref.shape[1] // leaf
    row = iota((rows, steps), 0)
    step = lax.axis_index("freq") * steps + iota((rows, steps), 1)
    freq = ((row >> 1) + total_freq // 2) % total_freq * (total_steps // total_freq) + 1
    phase = (freq * step + (row & 1) * (total_steps // 4)) & (total_steps - 1)
    angle = 2.0 * math.pi / total_steps * phase.astype(jnp.float32)
    damping = jnp.exp(step.astype(jnp.float32) * (math.log(fall_total) / total_steps))
    weights = (damping * jnp.cos(angle) / math.sqrt(total_steps)).astype(jnp.bfloat16)
    for copy in copies:
        copy.wait()
    part = dot(weights, history_ref[...])
    for l in range(leaves):
        out_ref[pl.ds(l, rows, stride=leaves), :] = part[:, l * leaf : (l + 1) * leaf]
    plan(chips, pick_ref, *index_refs)


def block_kernel(tasks, pick_ref, gathered_ref, right_ref, left_ref, blocks_ref, out_ref, near_ref):
    columns = gathered_ref.shape[0]
    picked = dot(pick_ref[:, :columns], gathered_ref[...])
    extra = pick_ref[: out_ref.shape[0], columns:].astype(jnp.float32)
    leaf = left_ref.shape[-1]
    own = iota((TILE, leaf), 0) % GROUP
    lane = iota((TILE, leaf), 1).astype(jnp.float32)
    leaves, near = blocks_ref.shape[:2]
    views = [
        picked[out_ref.shape[0] + TILE * n : out_ref.shape[0] + TILE * (n + 1)].astype(jnp.bfloat16)
        for n in range(near)
    ]

    def near_part(n):
        kept = jnp.zeros((TILE, 2 * leaf), jnp.float32)
        wide_own = iota((TILE, 2 * leaf), 0) % GROUP
        for l in range(leaves):
            kept = jnp.where(wide_own == l, dot(views[n], blocks_ref[l, n], True), kept)
        return kept

    groups = [
        (slice(2 * start, 2 * start + TILE), start, min(start + GROUP, tasks))
        for start in range(0, tasks, GROUP)
    ]
    coeffs, near_sums = [], near_part(0)
    for rows, start, stop in groups:
        coeff = jnp.zeros((TILE, leaf), jnp.float32)
        pair = jnp.concatenate([picked[rows], times_i(picked[rows])], 1).astype(jnp.bfloat16)
        for t in range(start, stop):
            coeff = jnp.where(own == t - start, dot(pair, right_ref[t]), coeff)
        coeffs.append(jnp.where(lane < extra[rows, :leaf], coeff, 0.0).astype(jnp.bfloat16))
    for n in range(1, near):
        near_sums = near_sums + near_part(n)
    for (rows, start, stop), coeff in zip(groups, coeffs):
        direct = jnp.zeros((TILE, leaf), jnp.float32)
        crossed = jnp.zeros((TILE, leaf), jnp.float32)
        for t in range(start, stop):
            both = dot(coeff, left_ref[t], True)
            direct = jnp.where(own == t - start, both[:, :leaf], direct)
            crossed = jnp.where(own == t - start, both[:, leaf:], crossed)
        terms = direct + times_i(crossed) + extra[rows, leaf:]
        out_ref[rows, :] = terms.astype(jnp.bfloat16)
    near_ref[...] = near_sums[:, :leaf] + times_i(near_sums[:, leaf:])


def spectrum_kernel(shares_ref, out_ref):
    spectrum = jnp.sum(shares_ref[...], 0).astype(jnp.bfloat16)
    for chip in range(out_ref.shape[0]):
        out_ref[chip] = spectrum


def field_kernel(arrived_ref, near_ref, out_ref):
    total = near_ref[...] + jnp.sum(arrived_ref[...].astype(jnp.float32), 0)
    parts = [
        jnp.concatenate([total[l : l + 1], total[GROUP + l : GROUP + l + 1]], 0)
        for l in range(GROUP)
    ]
    out_ref[...] = jnp.concatenate(parts, 1).astype(jnp.bfloat16)


def scatter_kernel(tasks, chips, terms_ref, out_ref):
    terms = terms_ref[...]
    columns = terms.shape[0]
    rows = columns // CORES
    spare = tasks // GROUP * TILE + tasks % GROUP
    lane = iota((1, terms.shape[1]), 1)
    wide = terms.astype(jnp.float32)

    def along(at):
        return jnp.where(lane < rows, wide[at : at + 1], wide[rows + at : rows + at + 1])

    goal = (along(spare) * GROUP + along(spare + 1)).astype(jnp.int32)
    code = (goal * 2 + lane // GROUP % 2)[:, :columns]
    row = iota((TILE, columns), 0)
    base = (lax.axis_index("core") * GROUP + row % GROUP) * 2 + row // GROUP
    place = jnp.concatenate(
        [
            jnp.where(code - chip * (CORES * TILE) == base, 1.0, 0.0)
            for chip in rotated(chips, first_chip(chips))
        ],
        0,
    )
    out_ref[...] = dot(place.astype(jnp.bfloat16), terms).astype(jnp.bfloat16)


def call(kernel, outs, spaces, scratch=(), limit=16, flops=0):
    return pl.pallas_call(
        kernel,
        out_shape=[jax.ShapeDtypeStruct(shape, dtype) for shape, dtype in outs],
        in_specs=[pl.BlockSpec(memory_space=space) for space in spaces],
        out_specs=[pl.BlockSpec(memory_space=pltpu.VMEM) for _ in outs],
        scratch_shapes=scratch,
        cost_estimate=pl.CostEstimate(flops=flops, transcendentals=0, bytes_accessed=2**20),
        compiler_params=pltpu.CompilerParams(vmem_limit_bytes=limit * 2**20),
    )


def per_device(
    history, near_blocks, near_leaves, far_left, far_right, far_ranks, far_targets, far_sources
):
    vmem = pltpu.VMEM
    freq_groups = lax.axis_size("freq")
    chips = lax.axis_size("chip")
    total_freq = far_ranks.shape[0] * freq_groups
    total_steps = history.shape[0] * freq_groups
    leaf = near_blocks.shape[-1]
    leaves = near_blocks.shape[1]
    near = near_blocks.shape[2]
    tasks = far_ranks.shape[1]
    slots = -(-tasks // GROUP) * GROUP

    arrays = (
        history,
        far_sources.reshape(1, tasks),
        far_ranks,
        far_targets.reshape(1, tasks),
        near_leaves.T,
    )
    partial, pick = call(
        functools.partial(partial_kernel, total_freq, total_steps, chips),
        [
            ((total_freq * TILE, leaf), jnp.float32),
            ((2 * slots + near * TILE, CORES * chips * TILE + 2 * LANES), jnp.bfloat16),
        ],
        [pl.ANY] * len(arrays),
        [
            *[pltpu.VMEM(array.shape, array.dtype) for array in arrays],
            pltpu.SemaphoreType.DMA((len(arrays),)),
        ],
    )(*[pltpu.with_memory_space_constraint(array, pltpu.HBM) for array in arrays])
    shares = lax.all_to_all(
        partial.reshape(total_freq, TILE, leaf),
        "freq",
        0,
        0,
        axis_index_groups=[rotated(freq_groups, freq_groups // 2)],
        tiled=True,
    )
    (copies,) = call(
        spectrum_kernel, [((chips, TILE, leaf), jnp.bfloat16)], [vmem], flops=20_000_000_000
    )(shares)
    same_core = lax.all_to_all(
        copies, "chip", 0, 0, axis_index_groups=[rotated(chips, first_chip(chips))], tiled=True
    )
    gathered = lax.all_gather(same_core, "core", axis=0, tiled=False)
    gathered = gathered.reshape(CORES * chips * TILE, leaf)

    terms, near_field = call(
        functools.partial(block_kernel, tasks),
        [((2 * slots, leaf), jnp.bfloat16), ((TILE, leaf), jnp.float32)],
        [vmem] * 5,
    )(
        pick,
        gathered,
        far_right[0].reshape(tasks, 2 * leaf, leaf),
        far_left[0].reshape(tasks, 2 * leaf, leaf),
        near_blocks[0].reshape(leaves, near, 2 * leaf, leaf),
    )

    both_terms = lax.all_gather(terms, "core", axis=0, tiled=True)
    (spread,) = call(
        functools.partial(scatter_kernel, tasks, chips),
        [((chips * TILE, leaf), jnp.bfloat16)],
        [vmem],
    )(both_terms)
    arrived = lax.all_to_all(
        spread.reshape(chips, TILE, leaf),
        "chip",
        0,
        0,
        axis_index_groups=[rotated(chips, first_chip(chips))],
        tiled=True,
    )

    (field,) = call(field_kernel, [((2, leaves * leaf), jnp.bfloat16)], [vmem, vmem])(
        arrived, near_field
    )
    return field[None]


def solution(mesh):
    freq_groups, elem_groups = mesh.devices.shape
    split = Mesh(
        mesh.devices.reshape(freq_groups, elem_groups // CORES, CORES), ("freq", "chip", "core")
    )
    elem = ("chip", "core")
    in_specs = (
        P("freq", elem),
        P("freq", elem, None, None, None, None),
        P(elem, None),
        P("freq", elem, None, None, None),
        P("freq", elem, None, None, None),
        P("freq", elem),
        P(elem),
        P(elem),
    )
    out_specs = P("freq", None, elem)
    return jax.shard_map(
        per_device, mesh=split, in_specs=in_specs, out_specs=out_specs, check_vma=False
    )
```

```python
import functools
import math

import jax
import jax.numpy as jnp
from jax import lax
from jax.experimental import pallas as pl
from jax.experimental.pallas import tpu as pltpu
from jax.sharding import Mesh
from jax.sharding import PartitionSpec as P

fall_total = 0.25
CORES = 2
GROUP = 8
TILE = 2 * GROUP
LANES = 128


def rotated(size, first):
    return [(i + first) % size for i in range(size)]


def chip_at(place, chips):
    return (place * 5 + chips - 2) % chips


def chip_order(chips):
    return [chip_at(place, chips) for place in range(chips)]


def dot(first_op, second_op, transposed=False):
    dims = (((1,), (1 if transposed else 0,)), ((), ()))
    return lax.dot_general(first_op, second_op, dims, preferred_element_type=jnp.float32)


def iota(shape, dim):
    return lax.broadcasted_iota(jnp.int32, shape, dim)


def times_i(tile):
    return jnp.concatenate([-tile[GROUP:], tile[:GROUP]], 0)


def leaf_codes(chunk, chips):
    at = chunk * LANES + iota((1, LANES), 1)
    core = at // (chips * TILE)
    chip = chip_at(at // TILE % chips, chips)
    return (chip * CORES + core) * TILE + at % GROUP * 2 + at // GROUP % 2


def plan(chips, pick_ref, sources_ref, ranks_ref, targets_ref, leaves_ref):
    tasks = sources_ref.shape[1]
    near, leaves = leaves_ref.shape
    rows = 2 * (-(-tasks // GROUP) * GROUP)
    row = iota((rows, LANES), 0)
    lane = iota((rows, LANES), 1)
    task = row // TILE * GROUP + row % GROUP
    part = row // GROUP % 2

    def by_row(ref):
        value = ref[...].astype(jnp.float32)
        found = jnp.where(iota((rows, tasks), 1) == task[:, :tasks], value, 0.0)
        return jnp.where(task < tasks, jnp.sum(found, 1, keepdims=True), -1.0)

    wanted = leaves_ref[...].astype(jnp.float32)
    own = iota((TILE, leaves), 1) == iota((TILE, leaves), 0) % GROUP
    listed = [
        jnp.sum(jnp.where(own, wanted[n : n + 1], 0.0), 1, keepdims=True) for n in range(near)
    ]
    near_part = iota((TILE, LANES), 0) // GROUP
    codes_of_rows = jnp.concatenate(
        [by_row(sources_ref).astype(jnp.int32) * 2 + part]
        + [leaf.astype(jnp.int32) * 2 + near_part for leaf in listed],
        0,
    )
    chunks = pick_ref.shape[1] // LANES - 2
    for chunk in range(chunks):
        pick_ref[:, chunk * LANES : (chunk + 1) * LANES] = jnp.where(
            codes_of_rows == leaf_codes(chunk, chips), 1.0, 0.0
        ).astype(jnp.bfloat16)
    target = jnp.sum(jnp.where(row == lane % rows, by_row(targets_ref), 0.0), 0, keepdims=True)
    target = target.astype(jnp.int32)
    spare = tasks // GROUP * TILE + tasks % GROUP
    goal = jnp.where(row == spare, target >> 3, jnp.where(row == spare + 1, target & 7, 0))
    extra = jnp.concatenate([by_row(ranks_ref), goal.astype(jnp.float32)], 1)
    pick_ref[:rows, chunks * LANES :] = extra.astype(jnp.bfloat16)
    pick_ref[rows:, chunks * LANES :] = jnp.zeros((near * TILE, 2 * LANES), jnp.bfloat16)


def partial_kernel(total_freq, total_steps, chips, *refs):
    count = (len(refs) - 3) // 2
    out_ref, pick_ref = refs[count : count + 2]
    history_ref, *index_refs = refs[count + 2 : -1]
    copies = [
        pltpu.make_async_copy(refs[i], refs[count + 2 + i], refs[-1].at[i]) for i in range(count)
    ]
    for copy in copies:
        copy.start()
    steps = history_ref.shape[0]
    rows = 2 * total_freq
    leaf = out_ref.shape[-1]
    leaves = history_ref.shape[1] // leaf
    row = iota((rows, steps), 0)
    step = lax.axis_index("freq") * steps + iota((rows, steps), 1)
    freq = ((row >> 1) + total_freq // 2) % total_freq * (total_steps // total_freq) + 1
    phase = (freq * step + (row & 1) * (total_steps // 4)) & (total_steps - 1)
    angle = 2.0 * math.pi / total_steps * phase.astype(jnp.float32)
    damping = jnp.exp(step.astype(jnp.float32) * (math.log(fall_total) / total_steps))
    weights = (damping * jnp.cos(angle) / math.sqrt(total_steps)).astype(jnp.bfloat16)
    for copy in copies:
        copy.wait()
    part = dot(weights, history_ref[...])
    for l in range(leaves):
        out_ref[pl.ds(l, rows, stride=leaves), :] = part[:, l * leaf : (l + 1) * leaf]
    plan(chips, pick_ref, *index_refs)


def block_kernel(tasks, pick_ref, gathered_ref, right_ref, left_ref, blocks_ref, out_ref, near_ref):
    columns = gathered_ref.shape[0]
    picked = dot(pick_ref[:, :columns], gathered_ref[...])
    extra = pick_ref[: out_ref.shape[0], columns:].astype(jnp.float32)
    leaf = left_ref.shape[-1]
    own = iota((TILE, leaf), 0) % GROUP
    lane = iota((TILE, leaf), 1).astype(jnp.float32)
    leaves, near = blocks_ref.shape[:2]
    views = [
        picked[out_ref.shape[0] + TILE * n : out_ref.shape[0] + TILE * (n + 1)].astype(jnp.bfloat16)
        for n in range(near)
    ]

    def near_part(n):
        kept = jnp.zeros((TILE, 2 * leaf), jnp.float32)
        wide_own = iota((TILE, 2 * leaf), 0) % GROUP
        for l in range(leaves):
            kept = jnp.where(wide_own == l, dot(views[n], blocks_ref[l, n], True), kept)
        return kept

    groups = [
        (slice(2 * start, 2 * start + TILE), start, min(start + GROUP, tasks))
        for start in range(0, tasks, GROUP)
    ]
    coeffs, near_sums = [], near_part(0)
    for rows, start, stop in groups:
        coeff = jnp.zeros((TILE, leaf), jnp.float32)
        pair = jnp.concatenate([picked[rows], times_i(picked[rows])], 1).astype(jnp.bfloat16)
        for t in range(start, stop):
            coeff = jnp.where(own == t - start, dot(pair, right_ref[t]), coeff)
        coeffs.append(jnp.where(lane < extra[rows, :leaf], coeff, 0.0).astype(jnp.bfloat16))
    for n in range(1, near):
        near_sums = near_sums + near_part(n)
    for (rows, start, stop), coeff in zip(groups, coeffs):
        direct = jnp.zeros((TILE, leaf), jnp.float32)
        crossed = jnp.zeros((TILE, leaf), jnp.float32)
        for t in range(start, stop):
            both = dot(coeff, left_ref[t], True)
            direct = jnp.where(own == t - start, both[:, :leaf], direct)
            crossed = jnp.where(own == t - start, both[:, leaf:], crossed)
        terms = direct + times_i(crossed) + extra[rows, leaf:]
        out_ref[rows, :] = terms.astype(jnp.bfloat16)
    near_ref[...] = near_sums[:, :leaf] + times_i(near_sums[:, leaf:])


def spectrum_kernel(shares_ref, out_ref):
    spectrum = jnp.sum(shares_ref[...], 0).astype(jnp.bfloat16)
    for chip in range(out_ref.shape[0]):
        out_ref[chip] = spectrum


def field_kernel(arrived_ref, near_ref, out_ref):
    total = near_ref[...] + jnp.sum(arrived_ref[...].astype(jnp.float32), 0)
    parts = [
        jnp.concatenate([total[l : l + 1], total[GROUP + l : GROUP + l + 1]], 0)
        for l in range(GROUP)
    ]
    out_ref[...] = jnp.concatenate(parts, 1).astype(jnp.bfloat16)


def scatter_kernel(tasks, chips, terms_ref, out_ref):
    terms = terms_ref[...]
    columns = terms.shape[0]
    rows = columns // CORES
    spare = tasks // GROUP * TILE + tasks % GROUP
    lane = iota((1, terms.shape[1]), 1)
    wide = terms.astype(jnp.float32)

    def along(at):
        return jnp.where(lane < rows, wide[at : at + 1], wide[rows + at : rows + at + 1])

    goal = (along(spare) * GROUP + along(spare + 1)).astype(jnp.int32)
    code = (goal * 2 + lane // GROUP % 2)[:, :columns]
    row = iota((TILE, columns), 0)
    base = (lax.axis_index("core") * GROUP + row % GROUP) * 2 + row // GROUP
    place = jnp.concatenate(
        [
            jnp.where(code - chip * (CORES * TILE) == base, 1.0, 0.0)
            for chip in chip_order(chips)
        ],
        0,
    )
    out_ref[...] = dot(place.astype(jnp.bfloat16), terms).astype(jnp.bfloat16)


def call(kernel, outs, spaces, scratch=(), limit=16, flops=0):
    return pl.pallas_call(
        kernel,
        out_shape=[jax.ShapeDtypeStruct(shape, dtype) for shape, dtype in outs],
        in_specs=[pl.BlockSpec(memory_space=space) for space in spaces],
        out_specs=[pl.BlockSpec(memory_space=pltpu.VMEM) for _ in outs],
        scratch_shapes=scratch,
        cost_estimate=pl.CostEstimate(flops=flops, transcendentals=0, bytes_accessed=2**20),
        compiler_params=pltpu.CompilerParams(vmem_limit_bytes=limit * 2**20),
    )


def per_device(
    history, near_blocks, near_leaves, far_left, far_right, far_ranks, far_targets, far_sources
):
    vmem = pltpu.VMEM
    freq_groups = lax.axis_size("freq")
    chips = lax.axis_size("chip")
    total_freq = far_ranks.shape[0] * freq_groups
    total_steps = history.shape[0] * freq_groups
    leaf = near_blocks.shape[-1]
    leaves = near_blocks.shape[1]
    near = near_blocks.shape[2]
    tasks = far_ranks.shape[1]
    slots = -(-tasks // GROUP) * GROUP

    arrays = (
        history,
        far_sources.reshape(1, tasks),
        far_ranks,
        far_targets.reshape(1, tasks),
        near_leaves.T,
    )
    partial, pick = call(
        functools.partial(partial_kernel, total_freq, total_steps, chips),
        [
            ((total_freq * TILE, leaf), jnp.float32),
            ((2 * slots + near * TILE, CORES * chips * TILE + 2 * LANES), jnp.bfloat16),
        ],
        [pl.ANY] * len(arrays),
        [
            *[pltpu.VMEM(array.shape, array.dtype) for array in arrays],
            pltpu.SemaphoreType.DMA((len(arrays),)),
        ],
    )(*[pltpu.with_memory_space_constraint(array, pltpu.HBM) for array in arrays])
    shares = lax.all_to_all(
        partial.reshape(total_freq, TILE, leaf),
        "freq",
        0,
        0,
        axis_index_groups=[rotated(freq_groups, freq_groups // 2)],
        tiled=True,
    )
    (copies,) = call(
        spectrum_kernel, [((chips, TILE, leaf), jnp.bfloat16)], [vmem], flops=20_000_000_000
    )(shares)
    same_core = lax.all_to_all(
        copies, "chip", 0, 0, axis_index_groups=[chip_order(chips)], tiled=True
    )
    gathered = lax.all_gather(same_core, "core", axis=0, tiled=False)
    gathered = gathered.reshape(CORES * chips * TILE, leaf)

    terms, near_field = call(
        functools.partial(block_kernel, tasks),
        [((2 * slots, leaf), jnp.bfloat16), ((TILE, leaf), jnp.float32)],
        [vmem] * 5,
    )(
        pick,
        gathered,
        far_right[0].reshape(tasks, 2 * leaf, leaf),
        far_left[0].reshape(tasks, 2 * leaf, leaf),
        near_blocks[0].reshape(leaves, near, 2 * leaf, leaf),
    )

    both_terms = lax.all_gather(terms, "core", axis=0, tiled=True)
    (spread,) = call(
        functools.partial(scatter_kernel, tasks, chips),
        [((chips * TILE, leaf), jnp.bfloat16)],
        [vmem],
    )(both_terms)
    arrived = lax.all_to_all(
        spread.reshape(chips, TILE, leaf),
        "chip",
        0,
        0,
        axis_index_groups=[chip_order(chips)],
        tiled=True,
    )

    (field,) = call(field_kernel, [((2, leaves * leaf), jnp.bfloat16)], [vmem, vmem])(
        arrived, near_field
    )
    return field[None]


def solution(mesh):
    freq_groups, elem_groups = mesh.devices.shape
    split = Mesh(
        mesh.devices.reshape(freq_groups, elem_groups // CORES, CORES), ("freq", "chip", "core")
    )
    elem = ("chip", "core")
    in_specs = (
        P("freq", elem),
        P("freq", elem, None, None, None, None),
        P(elem, None),
        P("freq", elem, None, None, None),
        P("freq", elem, None, None, None),
        P("freq", elem),
        P(elem),
        P(elem),
    )
    out_specs = P("freq", None, elem)
    return jax.shard_map(
        per_device, mesh=split, in_specs=in_specs, out_specs=out_specs, check_vma=False
    )
```

```python
import functools
import math

import jax
import jax.numpy as jnp
from jax import lax
from jax.experimental import pallas as pl
from jax.experimental.pallas import tpu as pltpu
from jax.sharding import Mesh
from jax.sharding import PartitionSpec as P

fall_total = 0.25
CORES = 2
GROUP = 8
TILE = 2 * GROUP
LANES = 128
GATHER_STRIDE, SUM_STRIDE = 23, 5


def rotated(size, first):
    return [(i + first) % size for i in range(size)]


def chip_at(place, chips, stride):
    return (place * stride + chips - 2) % chips


def chip_order(chips, stride):
    return [chip_at(place, chips, stride) for place in range(chips)]


def dot(first_op, second_op, transposed=False):
    dims = (((1,), (1 if transposed else 0,)), ((), ()))
    return lax.dot_general(first_op, second_op, dims, preferred_element_type=jnp.float32)


def iota(shape, dim):
    return lax.broadcasted_iota(jnp.int32, shape, dim)


def times_i(tile):
    return jnp.concatenate([-tile[GROUP:], tile[:GROUP]], 0)


def leaf_codes(chunk, chips):
    at = chunk * LANES + iota((1, LANES), 1)
    core = at // (chips * TILE)
    chip = chip_at(at // TILE % chips, chips, GATHER_STRIDE)
    return (chip * CORES + core) * TILE + at % GROUP * 2 + at // GROUP % 2


def plan(chips, pick_ref, sources_ref, ranks_ref, targets_ref, leaves_ref):
    tasks = sources_ref.shape[1]
    near, leaves = leaves_ref.shape
    rows = 2 * (-(-tasks // GROUP) * GROUP)
    row = iota((rows, LANES), 0)
    lane = iota((rows, LANES), 1)
    task = row // TILE * GROUP + row % GROUP
    part = row // GROUP % 2

    def by_row(ref):
        value = ref[...].astype(jnp.float32)
        found = jnp.where(iota((rows, tasks), 1) == task[:, :tasks], value, 0.0)
        return jnp.where(task < tasks, jnp.sum(found, 1, keepdims=True), -1.0)

    wanted = leaves_ref[...].astype(jnp.float32)
    own = iota((TILE, leaves), 1) == iota((TILE, leaves), 0) % GROUP
    listed = [
        jnp.sum(jnp.where(own, wanted[n : n + 1], 0.0), 1, keepdims=True) for n in range(near)
    ]
    near_part = iota((TILE, LANES), 0) // GROUP
    codes_of_rows = jnp.concatenate(
        [by_row(sources_ref).astype(jnp.int32) * 2 + part]
        + [leaf.astype(jnp.int32) * 2 + near_part for leaf in listed],
        0,
    )
    chunks = pick_ref.shape[1] // LANES - 2
    for chunk in range(chunks):
        pick_ref[:, chunk * LANES : (chunk + 1) * LANES] = jnp.where(
            codes_of_rows == leaf_codes(chunk, chips), 1.0, 0.0
        ).astype(jnp.bfloat16)
    target = jnp.sum(jnp.where(row == lane % rows, by_row(targets_ref), 0.0), 0, keepdims=True)
    target = target.astype(jnp.int32)
    spare = tasks // GROUP * TILE + tasks % GROUP
    goal = jnp.where(row == spare, target >> 3, jnp.where(row == spare + 1, target & 7, 0))
    extra = jnp.concatenate([by_row(ranks_ref), goal.astype(jnp.float32)], 1)
    pick_ref[:rows, chunks * LANES :] = extra.astype(jnp.bfloat16)
    pick_ref[rows:, chunks * LANES :] = jnp.zeros((near * TILE, 2 * LANES), jnp.bfloat16)


def partial_kernel(total_freq, total_steps, chips, *refs):
    count = (len(refs) - 3) // 2
    out_ref, pick_ref = refs[count : count + 2]
    history_ref, *index_refs = refs[count + 2 : -1]
    copies = [
        pltpu.make_async_copy(refs[i], refs[count + 2 + i], refs[-1].at[i]) for i in range(count)
    ]
    for copy in copies:
        copy.start()
    steps = history_ref.shape[0]
    rows = 2 * total_freq
    leaf = out_ref.shape[-1]
    leaves = history_ref.shape[1] // leaf
    row = iota((rows, steps), 0)
    step = lax.axis_index("freq") * steps + iota((rows, steps), 1)
    freq = ((row >> 1) + total_freq // 2) % total_freq * (total_steps // total_freq) + 1
    phase = (freq * step + (row & 1) * (total_steps // 4)) & (total_steps - 1)
    angle = 2.0 * math.pi / total_steps * phase.astype(jnp.float32)
    damping = jnp.exp(step.astype(jnp.float32) * (math.log(fall_total) / total_steps))
    weights = (damping * jnp.cos(angle) / math.sqrt(total_steps)).astype(jnp.bfloat16)
    for copy in copies:
        copy.wait()
    part = dot(weights, history_ref[...])
    for l in range(leaves):
        out_ref[pl.ds(l, rows, stride=leaves), :] = part[:, l * leaf : (l + 1) * leaf]
    plan(chips, pick_ref, *index_refs)


def block_kernel(tasks, pick_ref, gathered_ref, right_ref, left_ref, blocks_ref, out_ref, near_ref):
    columns = gathered_ref.shape[0]
    picked = dot(pick_ref[:, :columns], gathered_ref[...])
    extra = pick_ref[: out_ref.shape[0], columns:].astype(jnp.float32)
    leaf = left_ref.shape[-1]
    own = iota((TILE, leaf), 0) % GROUP
    lane = iota((TILE, leaf), 1).astype(jnp.float32)
    leaves, near = blocks_ref.shape[:2]
    views = [
        picked[out_ref.shape[0] + TILE * n : out_ref.shape[0] + TILE * (n + 1)].astype(jnp.bfloat16)
        for n in range(near)
    ]

    def near_part(n):
        kept = jnp.zeros((TILE, 2 * leaf), jnp.float32)
        wide_own = iota((TILE, 2 * leaf), 0) % GROUP
        for l in range(leaves):
            kept = jnp.where(wide_own == l, dot(views[n], blocks_ref[l, n], True), kept)
        return kept

    groups = [
        (slice(2 * start, 2 * start + TILE), start, min(start + GROUP, tasks))
        for start in range(0, tasks, GROUP)
    ]
    coeffs, near_sums = [], near_part(0)
    for rows, start, stop in groups:
        coeff = jnp.zeros((TILE, leaf), jnp.float32)
        pair = jnp.concatenate([picked[rows], times_i(picked[rows])], 1).astype(jnp.bfloat16)
        for t in range(start, stop):
            coeff = jnp.where(own == t - start, dot(pair, right_ref[t]), coeff)
        coeffs.append(jnp.where(lane < extra[rows, :leaf], coeff, 0.0).astype(jnp.bfloat16))
    for n in range(1, near):
        near_sums = near_sums + near_part(n)
    for (rows, start, stop), coeff in zip(groups, coeffs):
        direct = jnp.zeros((TILE, leaf), jnp.float32)
        crossed = jnp.zeros((TILE, leaf), jnp.float32)
        for t in range(start, stop):
            both = dot(coeff, left_ref[t], True)
            direct = jnp.where(own == t - start, both[:, :leaf], direct)
            crossed = jnp.where(own == t - start, both[:, leaf:], crossed)
        terms = direct + times_i(crossed) + extra[rows, leaf:]
        out_ref[rows, :] = terms.astype(jnp.bfloat16)
    near_ref[...] = near_sums[:, :leaf] + times_i(near_sums[:, leaf:])


def spectrum_kernel(shares_ref, out_ref):
    spectrum = jnp.sum(shares_ref[...], 0).astype(jnp.bfloat16)
    for chip in range(out_ref.shape[0]):
        out_ref[chip] = spectrum


def field_kernel(arrived_ref, near_ref, out_ref):
    total = near_ref[...] + jnp.sum(arrived_ref[...].astype(jnp.float32), 0)
    parts = [
        jnp.concatenate([total[l : l + 1], total[GROUP + l : GROUP + l + 1]], 0)
        for l in range(GROUP)
    ]
    out_ref[...] = jnp.concatenate(parts, 1).astype(jnp.bfloat16)


def scatter_kernel(tasks, chips, terms_ref, out_ref):
    terms = terms_ref[...]
    columns = terms.shape[0]
    rows = columns // CORES
    spare = tasks // GROUP * TILE + tasks % GROUP
    lane = iota((1, terms.shape[1]), 1)
    wide = terms.astype(jnp.float32)

    def along(at):
        return jnp.where(lane < rows, wide[at : at + 1], wide[rows + at : rows + at + 1])

    goal = (along(spare) * GROUP + along(spare + 1)).astype(jnp.int32)
    code = (goal * 2 + lane // GROUP % 2)[:, :columns]
    row = iota((TILE, columns), 0)
    base = (lax.axis_index("core") * GROUP + row % GROUP) * 2 + row // GROUP
    place = jnp.concatenate(
        [
            jnp.where(code - chip * (CORES * TILE) == base, 1.0, 0.0)
            for chip in chip_order(chips, SUM_STRIDE)
        ],
        0,
    )
    out_ref[...] = dot(place.astype(jnp.bfloat16), terms).astype(jnp.bfloat16)


def call(kernel, outs, spaces, scratch=(), limit=16, flops=0):
    return pl.pallas_call(
        kernel,
        out_shape=[jax.ShapeDtypeStruct(shape, dtype) for shape, dtype in outs],
        in_specs=[pl.BlockSpec(memory_space=space) for space in spaces],
        out_specs=[pl.BlockSpec(memory_space=pltpu.VMEM) for _ in outs],
        scratch_shapes=scratch,
        cost_estimate=pl.CostEstimate(flops=flops, transcendentals=0, bytes_accessed=2**20),
        compiler_params=pltpu.CompilerParams(vmem_limit_bytes=limit * 2**20),
    )


def per_device(
    history, near_blocks, near_leaves, far_left, far_right, far_ranks, far_targets, far_sources
):
    vmem = pltpu.VMEM
    freq_groups = lax.axis_size("freq")
    chips = lax.axis_size("chip")
    total_freq = far_ranks.shape[0] * freq_groups
    total_steps = history.shape[0] * freq_groups
    leaf = near_blocks.shape[-1]
    leaves = near_blocks.shape[1]
    near = near_blocks.shape[2]
    tasks = far_ranks.shape[1]
    slots = -(-tasks // GROUP) * GROUP

    arrays = (
        history,
        far_sources.reshape(1, tasks),
        far_ranks,
        far_targets.reshape(1, tasks),
        near_leaves.T,
    )
    partial, pick = call(
        functools.partial(partial_kernel, total_freq, total_steps, chips),
        [
            ((total_freq * TILE, leaf), jnp.float32),
            ((2 * slots + near * TILE, CORES * chips * TILE + 2 * LANES), jnp.bfloat16),
        ],
        [pl.ANY] * len(arrays),
        [
            *[pltpu.VMEM(array.shape, array.dtype) for array in arrays],
            pltpu.SemaphoreType.DMA((len(arrays),)),
        ],
    )(*[pltpu.with_memory_space_constraint(array, pltpu.HBM) for array in arrays])
    shares = lax.all_to_all(
        partial.reshape(total_freq, TILE, leaf),
        "freq",
        0,
        0,
        axis_index_groups=[rotated(freq_groups, freq_groups // 2)],
        tiled=True,
    )
    (copies,) = call(
        spectrum_kernel, [((chips, TILE, leaf), jnp.bfloat16)], [vmem], flops=20_000_000_000
    )(shares)
    same_core = lax.all_to_all(
        copies, "chip", 0, 0, axis_index_groups=[chip_order(chips, GATHER_STRIDE)], tiled=True
    )
    gathered = lax.all_gather(same_core, "core", axis=0, tiled=False)
    gathered = gathered.reshape(CORES * chips * TILE, leaf)

    terms, near_field = call(
        functools.partial(block_kernel, tasks),
        [((2 * slots, leaf), jnp.bfloat16), ((TILE, leaf), jnp.float32)],
        [vmem] * 5,
    )(
        pick,
        gathered,
        far_right[0].reshape(tasks, 2 * leaf, leaf),
        far_left[0].reshape(tasks, 2 * leaf, leaf),
        near_blocks[0].reshape(leaves, near, 2 * leaf, leaf),
    )

    both_terms = lax.all_gather(terms, "core", axis=0, tiled=True)
    (spread,) = call(
        functools.partial(scatter_kernel, tasks, chips),
        [((chips * TILE, leaf), jnp.bfloat16)],
        [vmem],
    )(both_terms)
    arrived = lax.all_to_all(
        spread.reshape(chips, TILE, leaf),
        "chip",
        0,
        0,
        axis_index_groups=[chip_order(chips, SUM_STRIDE)],
        tiled=True,
    )

    (field,) = call(field_kernel, [((2, leaves * leaf), jnp.bfloat16)], [vmem, vmem])(
        arrived, near_field
    )
    return field[None]


def solution(mesh):
    freq_groups, elem_groups = mesh.devices.shape
    split = Mesh(
        mesh.devices.reshape(freq_groups, elem_groups // CORES, CORES), ("freq", "chip", "core")
    )
    elem = ("chip", "core")
    in_specs = (
        P("freq", elem),
        P("freq", elem, None, None, None, None),
        P(elem, None),
        P("freq", elem, None, None, None),
        P("freq", elem, None, None, None),
        P("freq", elem),
        P(elem),
        P(elem),
    )
    out_specs = P("freq", None, elem)
    return jax.shard_map(
        per_device, mesh=split, in_specs=in_specs, out_specs=out_specs, check_vma=False
    )
```

```python
import functools
import math

import jax
import jax.numpy as jnp
from jax import lax
from jax.experimental import pallas as pl
from jax.experimental.pallas import tpu as pltpu
from jax.sharding import Mesh
from jax.sharding import PartitionSpec as P

fall_total = 0.25
CORES = 2
GROUP = 8
TILE = 2 * GROUP
LANES = 128
PARTS = 4
GATHER_STRIDE, SUM_STRIDE = 23, 5


def rotated(size, first):
    return [(i + first) % size for i in range(size)]


def chip_at(place, chips, stride):
    return (place * stride + chips - 2) % chips


def chip_order(chips, stride):
    return [chip_at(place, chips, stride) for place in range(chips)]


def dot(first_op, second_op, transposed=False):
    dims = (((1,), (1 if transposed else 0,)), ((), ()))
    return lax.dot_general(first_op, second_op, dims, preferred_element_type=jnp.float32)


def iota(shape, dim):
    return lax.broadcasted_iota(jnp.int32, shape, dim)


def times_i(tile):
    return jnp.concatenate([-tile[GROUP:], tile[:GROUP]], 0)


def leaf_codes(chunk, chips):
    at = chunk * LANES + iota((1, LANES), 1)
    core = at // (chips * TILE)
    chip = chip_at(at // TILE % chips, chips, GATHER_STRIDE)
    return (chip * CORES + core) * TILE + at % GROUP * 2 + at // GROUP % 2


def plan(chips, pick_ref, sources_ref, ranks_ref, targets_ref, leaves_ref):
    tasks = sources_ref.shape[1]
    near, leaves = leaves_ref.shape
    rows = 2 * (-(-tasks // GROUP) * GROUP)
    row = iota((rows, LANES), 0)
    lane = iota((rows, LANES), 1)
    task = row // TILE * GROUP + row % GROUP
    part = row // GROUP % 2

    def by_row(ref):
        value = ref[...].astype(jnp.float32)
        found = jnp.where(iota((rows, tasks), 1) == task[:, :tasks], value, 0.0)
        return jnp.where(task < tasks, jnp.sum(found, 1, keepdims=True), -1.0)

    wanted = leaves_ref[...].astype(jnp.float32)
    own = iota((TILE, leaves), 1) == iota((TILE, leaves), 0) % GROUP
    listed = [
        jnp.sum(jnp.where(own, wanted[n : n + 1], 0.0), 1, keepdims=True) for n in range(near)
    ]
    near_part = iota((TILE, LANES), 0) // GROUP
    codes_of_rows = jnp.concatenate(
        [by_row(sources_ref).astype(jnp.int32) * 2 + part]
        + [leaf.astype(jnp.int32) * 2 + near_part for leaf in listed],
        0,
    )
    chunks = pick_ref.shape[1] // LANES - 2
    for chunk in range(chunks):
        pick_ref[:, chunk * LANES : (chunk + 1) * LANES] = jnp.where(
            codes_of_rows == leaf_codes(chunk, chips), 1.0, 0.0
        ).astype(jnp.bfloat16)
    target = jnp.sum(jnp.where(row == lane % rows, by_row(targets_ref), 0.0), 0, keepdims=True)
    target = target.astype(jnp.int32)
    spare = tasks // GROUP * TILE + tasks % GROUP
    goal = jnp.where(row == spare, target >> 3, jnp.where(row == spare + 1, target & 7, 0))
    extra = jnp.concatenate([by_row(ranks_ref), goal.astype(jnp.float32)], 1)
    pick_ref[:rows, chunks * LANES :] = extra.astype(jnp.bfloat16)
    pick_ref[rows:, chunks * LANES :] = jnp.zeros((near * TILE, 2 * LANES), jnp.bfloat16)


def partial_kernel(total_freq, total_steps, chips, *refs):
    count = (len(refs) - 3) // 2
    out_ref, pick_ref = refs[count : count + 2]
    history_ref, *index_refs = refs[count + 2 : -1]
    width = history_ref.shape[1] // PARTS
    columns = [pl.ds(part * width, width) for part in range(PARTS)]
    copies = [
        pltpu.make_async_copy(
            refs[0].at[:, columns[part]], history_ref.at[:, columns[part]], refs[-1].at[part]
        )
        for part in range(PARTS)
    ] + [
        pltpu.make_async_copy(refs[i], refs[count + 2 + i], refs[-1].at[PARTS + i - 1])
        for i in range(1, count)
    ]
    for copy in copies:
        copy.start()
    steps = history_ref.shape[0]
    rows = 2 * total_freq
    leaf = out_ref.shape[-1]
    leaves = history_ref.shape[1] // leaf
    row = iota((rows, steps), 0)
    step = lax.axis_index("freq") * steps + iota((rows, steps), 1)
    freq = ((row >> 1) + total_freq // 2) % total_freq * (total_steps // total_freq) + 1
    phase = (freq * step + (row & 1) * (total_steps // 4)) & (total_steps - 1)
    angle = 2.0 * math.pi / total_steps * phase.astype(jnp.float32)
    damping = jnp.exp(step.astype(jnp.float32) * (math.log(fall_total) / total_steps))
    weights = (damping * jnp.cos(angle) / math.sqrt(total_steps)).astype(jnp.bfloat16)
    for copy in copies:
        copy.wait()
    part = dot(weights, history_ref[...])
    for l in range(leaves):
        out_ref[pl.ds(l, rows, stride=leaves), :] = part[:, l * leaf : (l + 1) * leaf]
    plan(chips, pick_ref, *index_refs)


def block_kernel(tasks, pick_ref, gathered_ref, right_ref, left_ref, blocks_ref, out_ref, near_ref):
    columns = gathered_ref.shape[0]
    picked = dot(pick_ref[:, :columns], gathered_ref[...])
    extra = pick_ref[: out_ref.shape[0], columns:].astype(jnp.float32)
    leaf = left_ref.shape[-1]
    own = iota((TILE, leaf), 0) % GROUP
    lane = iota((TILE, leaf), 1).astype(jnp.float32)
    leaves, near = blocks_ref.shape[:2]
    views = [
        picked[out_ref.shape[0] + TILE * n : out_ref.shape[0] + TILE * (n + 1)].astype(jnp.bfloat16)
        for n in range(near)
    ]

    def near_part(n):
        kept = jnp.zeros((TILE, 2 * leaf), jnp.float32)
        wide_own = iota((TILE, 2 * leaf), 0) % GROUP
        for l in range(leaves):
            kept = jnp.where(wide_own == l, dot(views[n], blocks_ref[l, n], True), kept)
        return kept

    groups = [
        (slice(2 * start, 2 * start + TILE), start, min(start + GROUP, tasks))
        for start in range(0, tasks, GROUP)
    ]
    coeffs, near_sums = [], near_part(0)
    for rows, start, stop in groups:
        coeff = jnp.zeros((TILE, leaf), jnp.float32)
        pair = jnp.concatenate([picked[rows], times_i(picked[rows])], 1).astype(jnp.bfloat16)
        for t in range(start, stop):
            coeff = jnp.where(own == t - start, dot(pair, right_ref[t]), coeff)
        coeffs.append(jnp.where(lane < extra[rows, :leaf], coeff, 0.0).astype(jnp.bfloat16))
    for n in range(1, near):
        near_sums = near_sums + near_part(n)
    for (rows, start, stop), coeff in zip(groups, coeffs):
        direct = jnp.zeros((TILE, leaf), jnp.float32)
        crossed = jnp.zeros((TILE, leaf), jnp.float32)
        for t in range(start, stop):
            both = dot(coeff, left_ref[t], True)
            direct = jnp.where(own == t - start, both[:, :leaf], direct)
            crossed = jnp.where(own == t - start, both[:, leaf:], crossed)
        terms = direct + times_i(crossed) + extra[rows, leaf:]
        out_ref[rows, :] = terms.astype(jnp.bfloat16)
    near_ref[...] = near_sums[:, :leaf] + times_i(near_sums[:, leaf:])


def spectrum_kernel(shares_ref, out_ref):
    spectrum = jnp.sum(shares_ref[...], 0).astype(jnp.bfloat16)
    for chip in range(out_ref.shape[0]):
        out_ref[chip] = spectrum


def field_kernel(arrived_ref, near_ref, out_ref):
    total = near_ref[...] + jnp.sum(arrived_ref[...].astype(jnp.float32), 0)
    parts = [
        jnp.concatenate([total[l : l + 1], total[GROUP + l : GROUP + l + 1]], 0)
        for l in range(GROUP)
    ]
    out_ref[...] = jnp.concatenate(parts, 1).astype(jnp.bfloat16)


def scatter_kernel(tasks, chips, terms_ref, out_ref):
    terms = terms_ref[...]
    columns = terms.shape[0]
    rows = columns // CORES
    spare = tasks // GROUP * TILE + tasks % GROUP
    lane = iota((1, terms.shape[1]), 1)
    wide = terms.astype(jnp.float32)

    def along(at):
        return jnp.where(lane < rows, wide[at : at + 1], wide[rows + at : rows + at + 1])

    goal = (along(spare) * GROUP + along(spare + 1)).astype(jnp.int32)
    code = (goal * 2 + lane // GROUP % 2)[:, :columns]
    row = iota((TILE, columns), 0)
    base = (lax.axis_index("core") * GROUP + row % GROUP) * 2 + row // GROUP
    place = jnp.concatenate(
        [
            jnp.where(code - chip * (CORES * TILE) == base, 1.0, 0.0)
            for chip in chip_order(chips, SUM_STRIDE)
        ],
        0,
    )
    out_ref[...] = dot(place.astype(jnp.bfloat16), terms).astype(jnp.bfloat16)


def call(kernel, outs, spaces, scratch=(), limit=16, flops=0):
    return pl.pallas_call(
        kernel,
        out_shape=[jax.ShapeDtypeStruct(shape, dtype) for shape, dtype in outs],
        in_specs=[pl.BlockSpec(memory_space=space) for space in spaces],
        out_specs=[pl.BlockSpec(memory_space=pltpu.VMEM) for _ in outs],
        scratch_shapes=scratch,
        cost_estimate=pl.CostEstimate(flops=flops, transcendentals=0, bytes_accessed=2**20),
        compiler_params=pltpu.CompilerParams(vmem_limit_bytes=limit * 2**20),
    )


def per_device(
    history, near_blocks, near_leaves, far_left, far_right, far_ranks, far_targets, far_sources
):
    vmem = pltpu.VMEM
    freq_groups = lax.axis_size("freq")
    chips = lax.axis_size("chip")
    total_freq = far_ranks.shape[0] * freq_groups
    total_steps = history.shape[0] * freq_groups
    leaf = near_blocks.shape[-1]
    leaves = near_blocks.shape[1]
    near = near_blocks.shape[2]
    tasks = far_ranks.shape[1]
    slots = -(-tasks // GROUP) * GROUP

    arrays = (
        history,
        far_sources.reshape(1, tasks),
        far_ranks,
        far_targets.reshape(1, tasks),
        near_leaves.T,
    )
    partial, pick = call(
        functools.partial(partial_kernel, total_freq, total_steps, chips),
        [
            ((total_freq * TILE, leaf), jnp.float32),
            ((2 * slots + near * TILE, CORES * chips * TILE + 2 * LANES), jnp.bfloat16),
        ],
        [pl.ANY] * len(arrays),
        [
            *[pltpu.VMEM(array.shape, array.dtype) for array in arrays],
            pltpu.SemaphoreType.DMA((PARTS + len(arrays) - 1,)),
        ],
    )(*[pltpu.with_memory_space_constraint(array, pltpu.HBM) for array in arrays])
    shares = lax.all_to_all(
        partial.reshape(total_freq, TILE, leaf),
        "freq",
        0,
        0,
        axis_index_groups=[rotated(freq_groups, freq_groups // 2)],
        tiled=True,
    )
    (copies,) = call(
        spectrum_kernel, [((chips, TILE, leaf), jnp.bfloat16)], [vmem], flops=20_000_000_000
    )(shares)
    same_core = lax.all_to_all(
        copies, "chip", 0, 0, axis_index_groups=[chip_order(chips, GATHER_STRIDE)], tiled=True
    )
    gathered = lax.all_gather(same_core, "core", axis=0, tiled=False)
    gathered = gathered.reshape(CORES * chips * TILE, leaf)

    terms, near_field = call(
        functools.partial(block_kernel, tasks),
        [((2 * slots, leaf), jnp.bfloat16), ((TILE, leaf), jnp.float32)],
        [vmem] * 5,
    )(
        pick,
        gathered,
        far_right[0].reshape(tasks, 2 * leaf, leaf),
        far_left[0].reshape(tasks, 2 * leaf, leaf),
        near_blocks[0].reshape(leaves, near, 2 * leaf, leaf),
    )

    both_terms = lax.all_gather(terms, "core", axis=0, tiled=True)
    (spread,) = call(
        functools.partial(scatter_kernel, tasks, chips),
        [((chips * TILE, leaf), jnp.bfloat16)],
        [vmem],
    )(both_terms)
    arrived = lax.all_to_all(
        spread.reshape(chips, TILE, leaf),
        "chip",
        0,
        0,
        axis_index_groups=[chip_order(chips, SUM_STRIDE)],
        tiled=True,
    )

    (field,) = call(field_kernel, [((2, leaves * leaf), jnp.bfloat16)], [vmem, vmem])(
        arrived, near_field
    )
    return field[None]


def solution(mesh):
    freq_groups, elem_groups = mesh.devices.shape
    split = Mesh(
        mesh.devices.reshape(freq_groups, elem_groups // CORES, CORES), ("freq", "chip", "core")
    )
    elem = ("chip", "core")
    in_specs = (
        P("freq", elem),
        P("freq", elem, None, None, None, None),
        P(elem, None),
        P("freq", elem, None, None, None),
        P("freq", elem, None, None, None),
        P("freq", elem),
        P(elem),
        P(elem),
    )
    out_specs = P("freq", None, elem)
    return jax.shard_map(
        per_device, mesh=split, in_specs=in_specs, out_specs=out_specs, check_vma=False
    )
```

```python
import functools
import math

import jax
import jax.numpy as jnp
from jax import lax
from jax.experimental import pallas as pl
from jax.experimental.pallas import tpu as pltpu
from jax.sharding import Mesh
from jax.sharding import PartitionSpec as P

fall_total = 0.25
CORES = 2
GROUP = 8
TILE = 2 * GROUP
LANES = 128
PARTS = 4
GATHER_STRIDE, SUM_STRIDE = 23, 5


def rotated(size, first):
    return [(i + first) % size for i in range(size)]


def chip_at(place, chips, stride):
    return (place * stride + chips - 2) % chips


def chip_order(chips, stride):
    return [chip_at(place, chips, stride) for place in range(chips)]


def dot(first_op, second_op, transposed=False):
    dims = (((1,), (1 if transposed else 0,)), ((), ()))
    return lax.dot_general(first_op, second_op, dims, preferred_element_type=jnp.float32)


def iota(shape, dim):
    return lax.broadcasted_iota(jnp.int32, shape, dim)


def times_i(tile):
    return jnp.concatenate([-tile[GROUP:], tile[:GROUP]], 0)


def leaf_codes(chunk, chips):
    at = chunk * LANES + iota((1, LANES), 1)
    core = at // (chips * TILE)
    chip = chip_at(at // TILE % chips, chips, GATHER_STRIDE)
    return (chip * CORES + core) * TILE + at % GROUP * 2 + at // GROUP % 2


def plan(chips, pick_ref, sources_ref, ranks_ref, targets_ref, leaves_ref):
    tasks = sources_ref.shape[1]
    near, leaves = leaves_ref.shape
    rows = 2 * (-(-tasks // GROUP) * GROUP)
    row = iota((rows, LANES), 0)
    lane = iota((rows, LANES), 1)
    task = row // TILE * GROUP + row % GROUP
    part = row // GROUP % 2

    def by_row(ref):
        value = ref[...].astype(jnp.float32)
        found = jnp.where(iota((rows, tasks), 1) == task[:, :tasks], value, 0.0)
        return jnp.where(task < tasks, jnp.sum(found, 1, keepdims=True), -1.0)

    wanted = leaves_ref[...].astype(jnp.float32)
    own = iota((TILE, leaves), 1) == iota((TILE, leaves), 0) % GROUP
    listed = [
        jnp.sum(jnp.where(own, wanted[n : n + 1], 0.0), 1, keepdims=True) for n in range(near)
    ]
    near_part = iota((TILE, LANES), 0) // GROUP
    codes_of_rows = jnp.concatenate(
        [by_row(sources_ref).astype(jnp.int32) * 2 + part]
        + [leaf.astype(jnp.int32) * 2 + near_part for leaf in listed],
        0,
    )
    chunks = pick_ref.shape[1] // LANES - 2
    for chunk in range(chunks):
        pick_ref[:, chunk * LANES : (chunk + 1) * LANES] = jnp.where(
            codes_of_rows == leaf_codes(chunk, chips), 1.0, 0.0
        ).astype(jnp.bfloat16)
    target = jnp.sum(jnp.where(row == lane % rows, by_row(targets_ref), 0.0), 0, keepdims=True)
    target = target.astype(jnp.int32)
    spare = tasks // GROUP * TILE + tasks % GROUP
    goal = jnp.where(row == spare, target >> 3, jnp.where(row == spare + 1, target & 7, 0))
    extra = jnp.concatenate([by_row(ranks_ref), goal.astype(jnp.float32)], 1)
    pick_ref[:rows, chunks * LANES :] = extra.astype(jnp.bfloat16)


def partial_kernel(total_freq, total_steps, chips, *refs):
    count = (len(refs) - 3) // 2
    out_ref, pick_ref = refs[count : count + 2]
    history_ref, *index_refs = refs[count + 2 : -1]
    width = history_ref.shape[1] // PARTS
    columns = [pl.ds(part * width, width) for part in range(PARTS)]
    copies = [
        pltpu.make_async_copy(
            refs[0].at[:, columns[part]], history_ref.at[:, columns[part]], refs[-1].at[part]
        )
        for part in range(PARTS)
    ] + [
        pltpu.make_async_copy(refs[i], refs[count + 2 + i], refs[-1].at[PARTS + i - 1])
        for i in range(1, count)
    ]
    for copy in copies:
        copy.start()
    steps = history_ref.shape[0]
    rows = 2 * total_freq
    leaf = out_ref.shape[-1]
    leaves = history_ref.shape[1] // leaf
    row = iota((rows, steps), 0)
    step = lax.axis_index("freq") * steps + iota((rows, steps), 1)
    freq = ((row >> 1) + total_freq // 2) % total_freq * (total_steps // total_freq) + 1
    phase = (freq * step + (row & 1) * (total_steps // 4)) & (total_steps - 1)
    angle = 2.0 * math.pi / total_steps * phase.astype(jnp.float32)
    damping = jnp.exp(step.astype(jnp.float32) * (math.log(fall_total) / total_steps))
    weights = (damping * jnp.cos(angle) / math.sqrt(total_steps)).astype(jnp.bfloat16)
    for copy in copies:
        copy.wait()
    part = dot(weights, history_ref[...])
    for l in range(leaves):
        out_ref[pl.ds(l, rows, stride=leaves), :] = part[:, l * leaf : (l + 1) * leaf]
    plan(chips, pick_ref, *index_refs)


def block_kernel(tasks, pick_ref, gathered_ref, right_ref, left_ref, blocks_ref, out_ref, near_ref):
    columns = gathered_ref.shape[0]
    picked = dot(pick_ref[:, :columns], gathered_ref[...])
    extra = pick_ref[: out_ref.shape[0], columns:].astype(jnp.float32)
    leaf = left_ref.shape[-1]
    own = iota((TILE, leaf), 0) % GROUP
    lane = iota((TILE, leaf), 1).astype(jnp.float32)
    leaves, near = blocks_ref.shape[:2]
    views = [
        picked[out_ref.shape[0] + TILE * n : out_ref.shape[0] + TILE * (n + 1)].astype(jnp.bfloat16)
        for n in range(near)
    ]

    def near_part(n):
        kept = jnp.zeros((TILE, 2 * leaf), jnp.float32)
        wide_own = iota((TILE, 2 * leaf), 0) % GROUP
        for l in range(leaves):
            kept = jnp.where(wide_own == l, dot(views[n], blocks_ref[l, n], True), kept)
        return kept

    groups = [
        (slice(2 * start, 2 * start + TILE), start, min(start + GROUP, tasks))
        for start in range(0, tasks, GROUP)
    ]
    coeffs = []
    for rows, start, stop in groups:
        coeff = jnp.zeros((TILE, leaf), jnp.float32)
        pair = jnp.concatenate([picked[rows], times_i(picked[rows])], 1).astype(jnp.bfloat16)
        for t in range(start, stop):
            coeff = jnp.where(own == t - start, dot(pair, right_ref[t]), coeff)
        coeffs.append(jnp.where(lane < extra[rows, :leaf], coeff, 0.0).astype(jnp.bfloat16))
    near_sums = near_part(0)
    for n in range(1, near):
        near_sums = near_sums + near_part(n)
    for (rows, start, stop), coeff in zip(groups, coeffs):
        direct = jnp.zeros((TILE, leaf), jnp.float32)
        crossed = jnp.zeros((TILE, leaf), jnp.float32)
        for t in range(start, stop):
            both = dot(coeff, left_ref[t], True)
            direct = jnp.where(own == t - start, both[:, :leaf], direct)
            crossed = jnp.where(own == t - start, both[:, leaf:], crossed)
        terms = direct + times_i(crossed) + extra[rows, leaf:]
        out_ref[rows, :] = terms.astype(jnp.bfloat16)
    near_ref[...] = near_sums[:, :leaf] + times_i(near_sums[:, leaf:])


def spectrum_kernel(shares_ref, out_ref):
    spectrum = jnp.sum(shares_ref[...], 0).astype(jnp.bfloat16)
    for chip in range(out_ref.shape[0]):
        out_ref[chip] = spectrum


def field_kernel(arrived_ref, near_ref, out_ref):
    total = near_ref[...] + jnp.sum(arrived_ref[...].astype(jnp.float32), 0)
    parts = [
        jnp.concatenate([total[l : l + 1], total[GROUP + l : GROUP + l + 1]], 0)
        for l in range(GROUP)
    ]
    out_ref[...] = jnp.concatenate(parts, 1).astype(jnp.bfloat16)


def scatter_kernel(tasks, chips, terms_ref, out_ref):
    terms = terms_ref[...]
    columns = terms.shape[0]
    rows = columns // CORES
    spare = tasks // GROUP * TILE + tasks % GROUP
    lane = iota((1, terms.shape[1]), 1)
    wide = terms.astype(jnp.float32)

    def along(at):
        return jnp.where(lane < rows, wide[at : at + 1], wide[rows + at : rows + at + 1])

    goal = (along(spare) * GROUP + along(spare + 1)).astype(jnp.int32)
    code = (goal * 2 + lane // GROUP % 2)[:, :columns]
    row = iota((TILE, columns), 0)
    base = (lax.axis_index("core") * GROUP + row % GROUP) * 2 + row // GROUP
    place = jnp.concatenate(
        [
            jnp.where(code - chip * (CORES * TILE) == base, 1.0, 0.0)
            for chip in chip_order(chips, SUM_STRIDE)
        ],
        0,
    )
    out_ref[...] = dot(place.astype(jnp.bfloat16), terms).astype(jnp.bfloat16)


def call(kernel, outs, spaces, scratch=(), limit=16, flops=0):
    return pl.pallas_call(
        kernel,
        out_shape=[jax.ShapeDtypeStruct(shape, dtype) for shape, dtype in outs],
        in_specs=[pl.BlockSpec(memory_space=space) for space in spaces],
        out_specs=[pl.BlockSpec(memory_space=pltpu.VMEM) for _ in outs],
        scratch_shapes=scratch,
        cost_estimate=pl.CostEstimate(flops=flops, transcendentals=0, bytes_accessed=2**20),
        compiler_params=pltpu.CompilerParams(vmem_limit_bytes=limit * 2**20),
    )


def per_device(
    history, near_blocks, near_leaves, far_left, far_right, far_ranks, far_targets, far_sources
):
    vmem = pltpu.VMEM
    freq_groups = lax.axis_size("freq")
    chips = lax.axis_size("chip")
    total_freq = far_ranks.shape[0] * freq_groups
    total_steps = history.shape[0] * freq_groups
    leaf = near_blocks.shape[-1]
    leaves = near_blocks.shape[1]
    near = near_blocks.shape[2]
    tasks = far_ranks.shape[1]
    slots = -(-tasks // GROUP) * GROUP

    arrays = (
        history,
        far_sources.reshape(1, tasks),
        far_ranks,
        far_targets.reshape(1, tasks),
        near_leaves.T,
    )
    partial, pick = call(
        functools.partial(partial_kernel, total_freq, total_steps, chips),
        [
            ((total_freq * TILE, leaf), jnp.float32),
            ((2 * slots + near * TILE, CORES * chips * TILE + 2 * LANES), jnp.bfloat16),
        ],
        [pl.ANY] * len(arrays),
        [
            *[pltpu.VMEM(array.shape, array.dtype) for array in arrays],
            pltpu.SemaphoreType.DMA((PARTS + len(arrays) - 1,)),
        ],
    )(*[pltpu.with_memory_space_constraint(array, pltpu.HBM) for array in arrays])
    shares = lax.all_to_all(
        partial.reshape(total_freq, TILE, leaf),
        "freq",
        0,
        0,
        axis_index_groups=[rotated(freq_groups, freq_groups // 2)],
        tiled=True,
    )
    (copies,) = call(
        spectrum_kernel, [((chips, TILE, leaf), jnp.bfloat16)], [vmem], flops=20_000_000_000
    )(shares)
    same_core = lax.all_to_all(
        copies, "chip", 0, 0, axis_index_groups=[chip_order(chips, GATHER_STRIDE)], tiled=True
    )
    gathered = lax.all_gather(same_core, "core", axis=0, tiled=False)
    gathered = gathered.reshape(CORES * chips * TILE, leaf)

    terms, near_field = call(
        functools.partial(block_kernel, tasks),
        [((2 * slots, leaf), jnp.bfloat16), ((TILE, leaf), jnp.float32)],
        [vmem] * 5,
    )(
        pick,
        gathered,
        far_right[0].reshape(tasks, 2 * leaf, leaf),
        far_left[0].reshape(tasks, 2 * leaf, leaf),
        near_blocks[0].reshape(leaves, near, 2 * leaf, leaf),
    )

    both_terms = lax.all_gather(terms, "core", axis=0, tiled=True)
    (spread,) = call(
        functools.partial(scatter_kernel, tasks, chips),
        [((chips * TILE, leaf), jnp.bfloat16)],
        [vmem],
    )(both_terms)
    arrived = lax.all_to_all(
        spread.reshape(chips, TILE, leaf),
        "chip",
        0,
        0,
        axis_index_groups=[chip_order(chips, SUM_STRIDE)],
        tiled=True,
    )

    (field,) = call(field_kernel, [((2, leaves * leaf), jnp.bfloat16)], [vmem, vmem])(
        arrived, near_field
    )
    return field[None]


def solution(mesh):
    freq_groups, elem_groups = mesh.devices.shape
    split = Mesh(
        mesh.devices.reshape(freq_groups, elem_groups // CORES, CORES), ("freq", "chip", "core")
    )
    elem = ("chip", "core")
    in_specs = (
        P("freq", elem),
        P("freq", elem, None, None, None, None),
        P(elem, None),
        P("freq", elem, None, None, None),
        P("freq", elem, None, None, None),
        P("freq", elem),
        P(elem),
        P(elem),
    )
    out_specs = P("freq", None, elem)
    return jax.shard_map(
        per_device, mesh=split, in_specs=in_specs, out_specs=out_specs, check_vma=False
    )
```
